32 devices in a mesh: slab: 8 (over z, y), rock: 4 (over x, core).
Axes of the slice: x: 2, y: 2, z: 4, core: 2. Of those that a mesh axis runs over, the one named last changes fastest.
Arguments:
- strain: float32 [1024, 6, 2048], P('slab', None, 'rock'), may hold values from -6 to 6
- dest: int32 [2, 1024, 1], P(None, 'slab'), may hold values from 0 to 7; in each aligned block of 128 rows (0 to 127, 128 to 255, ..., all dimensions but the last counted through in order) at most 32 rows name the same one
- det_row: int32 [2, 1024], P(None, 'slab'), may hold values from 0 to 7
- dirs: float32 [2, 4, 6], replicated, may hold values from -2.5 to 2.5
- rock_angles: float32 [16], replicated, may hold values from -2 to 2
- resolution: bfloat16 [2048, 2048], P(None, 'rock'), may hold values from -0.125 to 0.125
Outputs:
- detector: float32 [2, 64, 16, 2048], P(None, 'slab', None, 'rock')
The draws below stay inside these ranges and needn't reach their ends.
Inputs may be any that keep to these rules, and one draw needn't show every extreme that they name: `dest`: within the 128 tiles of one index of slab, at one angle, at most 32 tiles name the same owner, a bound that some block reaches.
All inputs are finite; a program needn't handle non-finite values.
Results may differ from the reference program's by a relative error of at most 0.0003.
Values sent between devices are 32-bit elements; how exact they have to be, the bound alone decides.
No kernel may reach another device: no remote copies, remote signals or barrier semaphores. Data moves between devices by JAX's collectives and lax.ppermute only.
A program may use at most 128 MiB of HBM per device.

```python
import math
import jax
import jax.numpy as jnp
import numpy as np
from jax import lax

TILES_DEV = 128
PIX = 2048
DEPTH = 1
COMP = 6
QDIR = 4
RANG = 16
ROWS = 8
ANGLES = 2
CAP = 32
TILES = 1024
VOX = 2048
DROWS = 64
N_SLAB = 8


def touch_ends(array, own_key, smallest, largest):
    longest = array.shape.index(max(array.shape))
    spots = []
    for shift in (0, 1):
        where = [jax.random.randint(jax.random.fold_in(own_key, axis), (), 0, length) for axis, length in enumerate(array.shape)]
        where[longest] = (where[longest] + shift) % array.shape[longest]
        spots.append(tuple(where))
    return array.at[spots[0]].set(smallest).at[spots[1]].set(largest)


def block_scale(rng, extent, split, low, largest):
    def one(dim, blocks):
        heights = jax.random.uniform(jax.random.fold_in(jax.random.fold_in(rng, 6), dim), (blocks,), jnp.float32, low / len(split), largest / len(split))
        return jnp.repeat(jnp.exp(heights), extent[dim] // blocks).reshape((-1,) + (1,) * (len(extent) - dim - 1))

    factor_of = one(*split[0])
    for cut in split[1:]:
        factor_of = factor_of * one(*cut)
    return factor_of


def assign_block(rng, own, number, rows, number_of, top, bound, skew):
    ranking = jax.random.permutation(rng, number_of)
    crowded, usual = load_shares(number_of, rows * top, bound, skew, True), load_shares(number_of, rows * top, bound, skew, False)
    places = jnp.arange(number_of)

    def named(tallies, turn):
        used = int((tallies > 0).sum())
        fixed = max(1, used // 4)
        moved = fixed + (places - fixed + turn * (used - fixed)) % max(1, number_of - fixed)
        return jnp.zeros((number_of,), jnp.int32).at[ranking[jnp.where(places < fixed, places, moved)]].set(jnp.asarray(tallies, jnp.int32))

    tallies = jnp.where(number % 4 == 0, named(crowded, number // 4), named(usual, number - number // 4 - 1))
    mixed = jax.random.permutation(jax.random.fold_in(own, 3), number_of)
    donor, receiver = mixed[0:number_of // 2 * 2:2], mixed[1:number_of // 2 * 2:2]
    room = jnp.minimum(tallies[donor] - 1, bound - tallies[receiver]) // 2
    room = jnp.where((donor == ranking[0]) | (receiver == ranking[0]) | (tallies[receiver] == 0), 0, jnp.maximum(room, 0))
    moved = jax.random.randint(jax.random.fold_in(own, 4), (number_of // 2,), 0, 1 << 20) % (room + 1)
    tallies = tallies.at[donor].add(-moved).at[receiver].add(moved)
    items = jnp.searchsorted(jnp.cumsum(tallies), jnp.arange(rows * top), side="right").astype(jnp.int32)
    table = items.reshape(top, rows).T
    table = table[jax.random.permutation(jax.random.fold_in(own, 1), rows)]
    turn = jax.random.randint(jax.random.fold_in(own, 2), (rows, 1), 0, top)
    return jnp.take_along_axis(table, (jnp.arange(top)[None, :] + turn) % top, axis=1)


def load_shares(amount, total, limit, skew, full):
    portions = [(1 << 20) // math.isqrt(rank ** skew) + 1 for rank in range(1, amount + 1)]
    largest = limit if full else min(limit, max(-(-total // amount), total * portions[0] // sum(portions)))
    least = 1 if total - largest >= amount - 1 else 0
    holding, spare = [largest] + [least] * (amount - 1), total - largest - least * (amount - 1)
    while spare > 0:
        movable = [i for i in range(1, amount) if holding[i] < largest] or [i for i in range(1, amount) if holding[i] < limit]
        whole, budget = sum([portions[i] for i in movable]), spare
        for i in movable:
            more = min(limit - holding[i], max(1, budget * portions[i] // whole), spare)
            holding[i] = holding[i] + more
            spare = spare - more
    return np.array(holding)


def gaussian(rng, dims, width, most, cuts=(), dtype=jnp.bfloat16):
    values = width * jax.random.normal(rng, dims, jnp.float32)
    if cuts:
        values = values * block_scale(rng, dims, cuts, -0.22, 0.18)
    return jnp.clip(values, -most, most).astype(dtype)


def setup_inputs(seed: int = 0) -> dict:
    key_of = jax.random.split(jax.random.key(seed), 7)
    strain = gaussian(key_of[0], (TILES, COMP, VOX), 1.0, 6.0, ((0, 8), (2, 4)), jnp.float32)
    dest_keys = jax.random.split(jax.random.fold_in(key_of[1], 1), ANGLES * TILES // TILES_DEV)
    dest_turns = jax.random.permutation(jax.random.fold_in(key_of[1], 3), ANGLES * TILES // TILES_DEV)
    dest = jax.vmap(lambda own, number: assign_block(jax.random.fold_in(key_of[1], 2), own, number, TILES_DEV, N_SLAB, 1, CAP, 2))(dest_keys, dest_turns).reshape((ANGLES, TILES, 1))
    det_row = touch_ends(jax.random.randint(key_of[2], (ANGLES, TILES), 0, ROWS), jax.random.fold_in(key_of[2], 1), 0, ROWS - 1).astype(jnp.int32)
    dirs = gaussian(key_of[3], (ANGLES, QDIR, COMP), COMP ** -0.5, 2.5, (), jnp.float32)
    rock_angles = jnp.clip(jax.random.uniform(key_of[4], (RANG,), jnp.float32, -2.0, 2.0), -2.0, 2.0)
    resolution = gaussian(key_of[5], (PIX, PIX), PIX ** -0.5, 0.125, ((1, 4),))
    return dict(strain=strain, dest=dest, det_row=det_row, dirs=dirs, rock_angles=rock_angles, resolution=resolution)


def reference(strain, dest, det_row, dirs, rock_angles, resolution):
    norm = ROWS / (QDIR * DEPTH * TILES_DEV)
    blocks = strain.reshape(N_SLAB, TILES_DEV, COMP, VOX)
    spread = resolution.astype(jnp.float32)
    outputs = []
    for angle in range(ANGLES):
        target = (dest[angle, :, 0] * ROWS + det_row[angle]).astype(jnp.int32).reshape(N_SLAB, TILES_DEV)
        weights = dirs[angle]

        def step(carry, item):
            block, where = item
            proj = jnp.einsum("qc,tcv->tqv", weights, block, precision=lax.Precision.HIGHEST)
            expo = jnp.exp(-0.5 * (proj[:, :, None, :] - rock_angles[None, None, :, None]) ** 2)
            inten = jnp.sum(expo, axis=1).reshape(TILES_DEV, RANG, PIX, DEPTH).sum(axis=3)
            added = carry.at[where].add(inten.reshape(TILES_DEV, RANG * PIX))
            return added, None

        image, unused = lax.scan(step, jnp.zeros((DROWS, RANG * PIX), jnp.float32), (blocks, target))
        image = image.reshape(DROWS, RANG, PIX) * norm
        outputs.append(jnp.einsum("grp,pk->grk", image, spread, precision=lax.Precision.HIGHEST))
    return jnp.stack(outputs, axis=0)
```

```python
import functools
import math
import jax
import jax.numpy as jnp
from jax import lax
from jax.experimental import pallas as pl
from jax.experimental.pallas import tpu as pltpu
from jax.sharding import PartitionSpec as P

TILES_DEV = 128
DEPTH = 1
QDIR = 4
ROWS = 8
ANGLES = 2
LANES = 128
GROUP = 8
SCALE = math.sqrt(0.5 / math.log(2.0))


def by_tiles(strain, dest, det_row, dirs, rock_angles, resolution):
    slabs = lax.axis_size("slab")
    tiles_here = strain.shape[0]
    vox_here = strain.shape[2]
    pix_here = resolution.shape[1]
    depth = vox_here // pix_here
    capacity = 2 * tiles_here // slabs
    slots = slabs * capacity
    block_size = 64
    rocks = rock_angles.shape[0]
    qcount = dirs.shape[1]
    norm = ROWS / (QDIR * DEPTH * TILES_DEV)
    row_ids = jnp.arange(ROWS, dtype=jnp.float32)
    lower = lax.broadcasted_iota(jnp.int32, (tiles_here, tiles_here), 1) < lax.broadcasted_iota(
        jnp.int32, (tiles_here, tiles_here), 0
    )

    def add_block(total, item):
        proj_block, row_block = item
        inten = jnp.sum(
            jnp.exp(-0.5 * (proj_block[:, :, None, :] - rock_angles[None, None, :, None]) ** 2),
            axis=1,
        )
        summed = inten.reshape(block_size, rocks, pix_here, depth).sum(axis=3)
        onehot = (row_ids[:, None] == row_block[None, :]).astype(jnp.float32)
        added = jnp.dot(
            onehot, summed.reshape(block_size, rocks * pix_here), precision=lax.Precision.HIGHEST
        )
        return (total + added, None)

    images = []
    for angle in range(ANGLES):
        owner = dest[angle, :, 0]
        same = (owner[:, None] == owner[None, :]) & lower
        rank = jnp.sum(same.astype(jnp.int32), axis=1)
        slot = owner * capacity + rank
        row_send = (
            jnp.full((slots,), -1.0, jnp.float32).at[slot].set(det_row[angle].astype(jnp.float32))
        )
        row_send = row_send.reshape(slabs, capacity)
        weights = dirs[angle]
        local_proj = jnp.einsum("qc,tcv->tqv", weights, strain, precision=lax.Precision.HIGHEST)
        outgoing = jnp.zeros((slots, qcount, vox_here), jnp.float32).at[slot].set(local_proj)
        outgoing = outgoing.reshape(slabs, capacity, qcount, vox_here)
        arrived, arrived_rows = (
            lax.all_to_all(outgoing, "slab", split_axis=0, concat_axis=0, tiled=True),
            lax.all_to_all(row_send, "slab", split_axis=0, concat_axis=0, tiled=True),
        )
        proj = arrived.reshape(slots, qcount, vox_here)
        proj_blocks = proj.reshape(slots // block_size, block_size, qcount, vox_here)
        row_blocks = arrived_rows.reshape(slots // block_size, block_size)
        image, unused = lax.scan(
            add_block, jnp.zeros((ROWS, rocks * pix_here), jnp.float32), (proj_blocks, row_blocks)
        )
        images.append(image.reshape(ROWS, rocks, pix_here) * norm)
    stacked = jnp.stack(images, axis=0)
    columns = resolution.astype(jnp.float32)
    return jnp.einsum(
        "agrp,pk->agrk",
        lax.all_gather(stacked, "rock", axis=3, tiled=True),
        columns,
        precision=lax.Precision.HIGHEST,
    )


def image_kernel(count_ref, list_ref, dirs_ref, rock_ref, own_ref, other_ref, far_ref, near_ref, proj, acc):
    comps, tiles, lanes = own_ref.shape
    angles = count_ref.shape[0]
    qcount = dirs_ref.shape[0] // (angles * comps)
    rocks = rock_ref.shape[0]
    step = 2 * GROUP

    for half, ref in enumerate((own_ref, other_ref)):

        @pl.loop(0, tiles // step)
        def _(block):
            rows = pl.ds(pl.multiple_of(block * step, step), step)
            place = pl.ds(pl.multiple_of(half * tiles + block * step, step), step)
            parts = [ref[c, rows, :] for c in range(comps)]
            for k in range(angles * qcount):
                total = parts[0] * dirs_ref[k * comps]
                for c in range(1, comps):
                    total = total + parts[c] * dirs_ref[k * comps + c]
                proj[k, place, :] = total

    acc[...] = jnp.zeros_like(acc)
    rock = rock_ref[...]
    for angle in range(angles):

        @pl.loop(0, (count_ref[angle] + GROUP - 1) // GROUP)
        def _(block):
            sums = []
            targets = []
            for j in range(GROUP):
                code = list_ref[angle, block * GROUP + j]
                tile = code % (2 * tiles)
                targets.append(pl.multiple_of(code // (2 * tiles) * rocks, rocks))
                total = None
                for q in range(qcount):
                    p = proj[angle * qcount + q, pl.ds(tile, 1), :]
                    d = jnp.broadcast_to(p, (rocks, lanes)) - rock
                    e = jnp.exp2(-(d * d))
                    total = e if total is None else total + e
                sums.append(total)
            for target, total in zip(targets, sums):
                acc[pl.ds(target, rocks), :] += total

    near = near_ref.shape[0]
    far = far_ref.shape[0]
    far_ref[...] = acc[pl.ds(0, far), :]
    near_ref[...] = acc[pl.ds(far, near), :]


def partial_images(counts, lists, dirs, rock, own, other, line):
    comps, tiles, lanes = own.shape
    angles = counts.shape[0]
    qcount = dirs.shape[0] // (angles * comps)
    rocks = rock.shape[0]
    unit = angles * ROWS * rocks
    smem = pl.BlockSpec(memory_space=pltpu.SMEM)
    vmem = pl.BlockSpec(memory_space=pltpu.VMEM)
    return pl.pallas_call(
        image_kernel,
        out_shape=(
            jax.ShapeDtypeStruct(((line - 1) * unit, lanes), jnp.float32),
            jax.ShapeDtypeStruct((unit, lanes), jnp.float32),
        ),
        in_specs=[smem, smem, smem, vmem, vmem, vmem],
        out_specs=(vmem, vmem),
        scratch_shapes=[
            pltpu.VMEM((angles * qcount, 2 * tiles, lanes), jnp.float32),
            pltpu.VMEM((line * unit + rocks, lanes), jnp.float32),
        ],
        cost_estimate=pl.CostEstimate(flops=6_000_000, bytes_accessed=2_000_000, transcendentals=0),
        name="partial_images",
    )(counts, lists, dirs, rock, own, other)


def resolve_kernel(rock_ref, first, pix, norm, total_ref, res_ref, *rest):
    parts, out_ref = rest[:-1], rest[-1]
    lanes = parts[0].shape[1]
    total = total_ref[...] if total_ref is not None else None
    for j, part in enumerate(parts):
        start = pl.multiple_of((rock_ref[0] ^ j) * pix + first, lanes)
        block = res_ref[pl.ds(start, lanes), :]
        value = part[...] * norm
        high = value.astype(jnp.bfloat16)
        low = (value - high.astype(jnp.float32)).astype(jnp.bfloat16)
        added = jnp.dot(high, block, preferred_element_type=jnp.float32) + jnp.dot(
            low, block, preferred_element_type=jnp.float32
        )
        total = added if total is None else total + added
    out_ref[...] = total


def resolve(rock_index, first, pix, norm, total, resolution, parts):
    unit, lanes = parts[0].shape
    cols = resolution.shape[1]
    smem = pl.BlockSpec(memory_space=pltpu.SMEM)
    vmem = pl.BlockSpec(memory_space=pltpu.VMEM)

    def kernel(rock_ref, *refs):
        if total is None:
            resolve_kernel(rock_ref, first, pix, norm, None, *refs)
        else:
            resolve_kernel(rock_ref, first, pix, norm, *refs)

    before = () if total is None else (total,)
    return pl.pallas_call(
        kernel,
        out_shape=jax.ShapeDtypeStruct((unit, cols), jnp.float32),
        in_specs=[smem] + [vmem] * (len(before) + 1 + len(parts)),
        out_specs=vmem,
        cost_estimate=pl.CostEstimate(flops=500_000_000, bytes_accessed=3_000_000, transcendentals=0),
        name="resolve",
    )(rock_index, *before, resolution, *parts)


def line_sum(far, near, line, unit, pair):
    half = line // 2
    place = lax.axis_index("slab") // pair

    def send(value, links):
        pairs = [(a * pair + k, b * pair + k) for a, b in links for k in range(pair)]
        return lax.ppermute(value, "slab", pairs)

    held = far
    for p in range(half - 1):
        count = line - 1 - p
        arrived = send(held[: count * unit], [(p, p + 1), (line - 1 - p, line - 2 - p)])
        held = jnp.concatenate([held[: count * unit] + arrived, held[count * unit :]], axis=0)
    own = [held[j * unit : (j + 1) * unit] for j in range(line - 1)] + [near]
    middle = send(held[: half * unit], [(half - 1, half), (half, half - 1)])
    carried = [middle[j * unit : (j + 1) * unit] for j in range(half)]
    outer = []
    for p in range(half, line - 1):
        count = line - 1 - p
        sent = jnp.concatenate([own[line - 1 - j] + carried[j] for j in range(count)], axis=0)
        outer.append(sent)
        arrived = send(sent, [(p, p + 1), (line - 1 - p, line - 2 - p)])
        arrived = [arrived[j * unit : (j + 1) * unit] for j in range(count)]
        carried = [carried[j] + arrived[j] for j in range(count)] + carried[count:]
    fold = jnp.where(place < half, line - 1 - place, place)
    result = own[line - 1] + carried[0]
    for j in range(1, half):
        result = jnp.where(fold == line - 1 - j, own[line - 1 - j] + carried[j], result)
    return result


def by_images(strain, dest, det_row, dirs, rock_angles, resolution):
    slabs = lax.axis_size("slab")
    rock_size = lax.axis_size("rock")
    tiles = strain.shape[0]
    pix = resolution.shape[1]
    rocks = rock_angles.shape[0]
    angles, qcount, comps = dirs.shape
    norm = ROWS / (QDIR * DEPTH * TILES_DEV)
    pair = 2
    line = slabs // pair
    unit = angles * ROWS * rocks
    me = lax.axis_index("slab")
    swap = [(i, i ^ 1) for i in range(slabs)]
    chunks = pix // LANES

    info = dest[:, :, 0] * ROWS + det_row
    other_info = lax.ppermute(info, "slab", swap)
    by_comp = strain.transpose(1, 0, 2)
    own = [by_comp[:, :, c * LANES : (c + 1) * LANES] for c in range(chunks)]
    other = [lax.ppermute(own[c], "slab", swap) for c in range(chunks)]

    info = jnp.concatenate([info, other_info], axis=1)
    owner = info // ROWS
    place = owner // pair
    keep = owner % pair == me % pair
    position = jnp.where(me // pair < line // 2, line - 1 - place, place)
    target = (position * angles + jnp.arange(angles)[:, None]) * ROWS + info % ROWS
    number = jnp.arange(2 * tiles)
    earlier = keep[:, None, :] & (number[None, None, :] < number[None, :, None])
    rank = jnp.sum(earlier.astype(jnp.int32), axis=2)
    rank = jnp.where(keep, rank, -1)
    trash = line * angles * ROWS
    code = number[None, :] + 2 * tiles * (target - trash)
    lists = 2 * tiles * trash + jnp.sum(
        jnp.where(rank[:, None, :] == number[None, :, None], code[:, None, :], 0), axis=2
    )
    counts = jnp.sum(keep.astype(jnp.int32), axis=1)

    weights = (dirs * SCALE).reshape(-1)
    rock = jnp.broadcast_to((rock_angles * SCALE)[:, None], (rocks, LANES))
    rock_index = lax.axis_index("rock").reshape(1)

    result = None
    for c in range(chunks):
        far, near = partial_images(counts, lists, weights, rock, own[c], other[c], line)
        parts = [line_sum(far, near, line, unit, pair)]
        bit = rock_size // 2
        order = [0]
        while bit:
            links = [(i, i ^ bit) for i in range(rock_size)]
            parts = parts + [lax.ppermute(part, "rock", links) for part in parts]
            order = order + [k ^ bit for k in order]
            bit //= 2
        parts = [parts[order.index(k)] for k in range(rock_size)]
        result = resolve(rock_index, c * LANES, pix, norm, result, resolution, parts)
    return result.reshape(angles, ROWS, rocks, pix)


def local(strain, dest, det_row, dirs, rock_angles, resolution):
    slabs = lax.axis_size("slab")
    rock_size = lax.axis_size("rock")
    tiles, unused, vox = strain.shape
    pix = resolution.shape[1]
    slots = slabs * (2 * tiles // slabs)
    images_smaller = slabs * ROWS * rock_angles.shape[0] * pix <= slots * dirs.shape[1] * vox
    regular = slabs % 4 == 0 and rock_size & (rock_size - 1) == 0 and vox == pix and pix % LANES == 0
    plan = by_images if images_smaller and regular else by_tiles
    return plan(strain, dest, det_row, dirs, rock_angles, resolution)


def solution(mesh):
    placed = (
        P("slab", None, "rock"),
        P(None, "slab", None),
        P(None, "slab"),
        P(),
        P(),
        P(None, "rock"),
    )
    return jax.shard_map(
        local, mesh=mesh, in_specs=placed, out_specs=P(None, "slab", None, "rock"), check_vma=False
    )
```

```python
import math
import jax
import jax.numpy as jnp
from jax import lax
from jax.experimental import pallas as pl
from jax.experimental.pallas import tpu as pltpu
from jax.sharding import PartitionSpec as P

TILES_DEV = 128
DEPTH = 1
QDIR = 4
ROWS = 8
ANGLES = 2
LANES = 128
GROUP = 8
VMEM_LIMIT = 12 * 1024 * 1024
SCALE = math.sqrt(0.5 / math.log(2.0))


def by_tiles(strain, dest, det_row, dirs, rock_angles, resolution):
    slabs = lax.axis_size("slab")
    tiles_here = strain.shape[0]
    vox_here = strain.shape[2]
    pix_here = resolution.shape[1]
    depth = vox_here // pix_here
    capacity = 2 * tiles_here // slabs
    slots = slabs * capacity
    block_size = 64
    rocks = rock_angles.shape[0]
    qcount = dirs.shape[1]
    norm = ROWS / (QDIR * DEPTH * TILES_DEV)
    row_ids = jnp.arange(ROWS, dtype=jnp.float32)
    lower = lax.broadcasted_iota(jnp.int32, (tiles_here, tiles_here), 1) < lax.broadcasted_iota(
        jnp.int32, (tiles_here, tiles_here), 0
    )

    def add_block(total, item):
        proj_block, row_block = item
        inten = jnp.sum(
            jnp.exp(-0.5 * (proj_block[:, :, None, :] - rock_angles[None, None, :, None]) ** 2),
            axis=1,
        )
        summed = inten.reshape(block_size, rocks, pix_here, depth).sum(axis=3)
        onehot = (row_ids[:, None] == row_block[None, :]).astype(jnp.float32)
        added = jnp.dot(
            onehot, summed.reshape(block_size, rocks * pix_here), precision=lax.Precision.HIGHEST
        )
        return (total + added, None)

    images = []
    for angle in range(ANGLES):
        owner = dest[angle, :, 0]
        same = (owner[:, None] == owner[None, :]) & lower
        rank = jnp.sum(same.astype(jnp.int32), axis=1)
        slot = owner * capacity + rank
        row_send = (
            jnp.full((slots,), -1.0, jnp.float32).at[slot].set(det_row[angle].astype(jnp.float32))
        )
        row_send = row_send.reshape(slabs, capacity)
        weights = dirs[angle]
        local_proj = jnp.einsum("qc,tcv->tqv", weights, strain, precision=lax.Precision.HIGHEST)
        outgoing = jnp.zeros((slots, qcount, vox_here), jnp.float32).at[slot].set(local_proj)
        outgoing = outgoing.reshape(slabs, capacity, qcount, vox_here)
        arrived, arrived_rows = (
            lax.all_to_all(outgoing, "slab", split_axis=0, concat_axis=0, tiled=True),
            lax.all_to_all(row_send, "slab", split_axis=0, concat_axis=0, tiled=True),
        )
        proj = arrived.reshape(slots, qcount, vox_here)
        proj_blocks = proj.reshape(slots // block_size, block_size, qcount, vox_here)
        row_blocks = arrived_rows.reshape(slots // block_size, block_size)
        image, unused = lax.scan(
            add_block, jnp.zeros((ROWS, rocks * pix_here), jnp.float32), (proj_blocks, row_blocks)
        )
        images.append(image.reshape(ROWS, rocks, pix_here) * norm)
    stacked = jnp.stack(images, axis=0)
    columns = resolution.astype(jnp.float32)
    return jnp.einsum(
        "agrp,pk->agrk",
        lax.all_gather(stacked, "rock", axis=3, tiled=True),
        columns,
        precision=lax.Precision.HIGHEST,
    )


def image_kernel(count_ref, list_ref, dirs_ref, rock_ref, strain_ref, *rest):
    proj = rest[-1]
    comps, tiles, pix = strain_ref.shape
    angles = count_ref.shape[0]
    qcount = dirs_ref.shape[0] // (angles * comps)
    rocks = rock_ref.shape[0]
    step = 2 * GROUP
    if len(rest) == 2:
        init, outs = None, rest[:1]
    else:
        init, outs = rest[0], rest[1:-2]
    acc = outs[0] if init is None else rest[-2]
    blocks = pix // LANES
    rows_out = acc.shape[0] // blocks
    rock = rock_ref[...]
    if init is None:
        acc[...] = jnp.zeros_like(acc)
    else:
        acc[...] = init[...]

    for b in range(blocks):
        lanes = slice(b * LANES, (b + 1) * LANES)

        @pl.loop(0, tiles // step)
        def _(block):
            rows = pl.ds(pl.multiple_of(block * step, step), step)
            parts = [strain_ref[c, rows, lanes] for c in range(comps)]
            for k in range(angles * qcount):
                total = parts[0] * dirs_ref[k * comps]
                for c in range(1, comps):
                    total = total + parts[c] * dirs_ref[k * comps + c]
                proj[k, rows, :] = total

        for angle in range(angles):

            @pl.loop(0, (count_ref[angle] + GROUP - 1) // GROUP)
            def _(block):
                sums = []
                targets = []
                for j in range(GROUP):
                    code = list_ref[angle, block * GROUP + j]
                    tile = code & (tiles - 1)
                    target = (code >> (tiles - 1).bit_length()) * rocks
                    targets.append(pl.multiple_of(target + b * rows_out, rocks))
                    total = None
                    for q in range(qcount):
                        p = proj[angle * qcount + q, pl.ds(tile, 1), :]
                        d = jnp.broadcast_to(p, (rocks, LANES)) - rock
                        e = jnp.exp2(-(d * d))
                        total = e if total is None else total + e
                    sums.append(total)
                for target, total in zip(targets, sums):
                    acc[pl.ds(target, rocks), :] += total

    if init is not None:
        start = 0
        for out in outs:
            out[...] = acc[pl.ds(start, out.shape[0]), :]
            start += out.shape[0]


def add_images(name, listing, weights, rock, strain, init, sizes, cost):
    counts, lists = listing
    comps, tiles, pix = strain.shape
    angles = counts.shape[0]
    qcount = weights.shape[0] // (angles * comps)
    smem = pl.BlockSpec(memory_space=pltpu.SMEM)
    vmem = pl.BlockSpec(memory_space=pltpu.VMEM)
    scratch = [pltpu.VMEM((angles * qcount, tiles, LANES), jnp.float32)]
    before = ()
    if init is not None:
        before = (init,)
        scratch = [pltpu.VMEM(init.shape, jnp.float32)] + scratch
    return pl.pallas_call(
        image_kernel,
        out_shape=tuple(jax.ShapeDtypeStruct((size, LANES), jnp.float32) for size in sizes),
        in_specs=[smem, smem, smem] + [vmem] * (2 + len(before)),
        out_specs=tuple(vmem for size in sizes),
        scratch_shapes=scratch,
        compiler_params=pltpu.CompilerParams(vmem_limit_bytes=VMEM_LIMIT),
        cost_estimate=pl.CostEstimate(flops=cost, bytes_accessed=1_000_000, transcendentals=0),
        name=name,
    )(counts, lists, weights, rock, strain, *before)


def resolve(rock_index, firsts, pix, norm, total, resolution, parts):
    count = len(firsts)
    unit = parts[0].shape[0] // count
    lanes = parts[0].shape[1]
    cols = resolution.shape[1]
    smem = pl.BlockSpec(memory_space=pltpu.SMEM)
    vmem = pl.BlockSpec(memory_space=pltpu.VMEM)

    def kernel(rock_ref, res_ref, *refs):
        part_refs, out_ref = refs[: len(parts)], refs[-1]
        values = []
        blocks = []
        for j, part in enumerate(part_refs):
            for c, first in enumerate(firsts):
                start = pl.multiple_of((rock_ref[0] ^ j) * pix + first, lanes)
                blocks.append(res_ref[pl.ds(start, lanes), :])
                values.append(part[pl.ds(c * unit, unit), :] * norm)
        block = jnp.concatenate(blocks, axis=0)
        value = jnp.concatenate(values, axis=1)
        high = value.astype(jnp.bfloat16)
        low = (value - high.astype(jnp.float32)).astype(jnp.bfloat16)
        result = jnp.dot(high, block, preferred_element_type=jnp.float32) + jnp.dot(
            low, block, preferred_element_type=jnp.float32
        )
        if total is not None:
            result = result + refs[len(parts)][...]
        out_ref[...] = result

    before = () if total is None else (total,)
    return pl.pallas_call(
        kernel,
        out_shape=jax.ShapeDtypeStruct((unit, cols), jnp.float32),
        in_specs=[smem] + [vmem] * (1 + len(parts) + len(before)),
        out_specs=vmem,
        compiler_params=pltpu.CompilerParams(vmem_limit_bytes=VMEM_LIMIT),
        cost_estimate=pl.CostEstimate(flops=500_000_000, bytes_accessed=1_000_000, transcendentals=0),
        name="resolve",
    )(rock_index, resolution, *parts, *before)


def bit(value, number):
    return (value >> number) & 1


def listing(info, me, raw, halves, angles, units):
    tiles = info.shape[1]
    owner = info // ROWS
    keep = bit(owner, raw) == bit(me, raw)
    position = jnp.zeros_like(owner)
    for number in halves:
        position = 2 * position + (bit(owner, number) == bit(me, number)).astype(jnp.int32)
    target = (position * angles + jnp.arange(angles)[:, None]) * ROWS + info % ROWS
    number = jnp.arange(tiles)
    earlier = keep[:, None, :] & (number[None, None, :] < number[None, :, None])
    rank = jnp.where(keep, jnp.sum(earlier.astype(jnp.int32), axis=2), -1)
    code = number[None, :] + tiles * (target - units)
    lists = tiles * units + jnp.sum(
        jnp.where(rank[:, None, :] == number[None, :, None], code[:, None, :], 0), axis=2
    )
    return jnp.sum(keep.astype(jnp.int32), axis=1), lists


def by_images(strain, dest, det_row, dirs, rock_angles, resolution):
    slabs = lax.axis_size("slab")
    rock_size = lax.axis_size("rock")
    tiles = strain.shape[0]
    pix = resolution.shape[1]
    rocks = rock_angles.shape[0]
    angles, qcount, comps = dirs.shape
    norm = ROWS / (QDIR * DEPTH * TILES_DEV)
    bits = slabs.bit_length() - 1
    unit = angles * ROWS * rocks
    units = slabs // 2 * angles * ROWS
    image_rows = units * rocks
    me = lax.axis_index("slab")
    chunks = pix // LANES

    def swap(value, number, axis="slab"):
        size = lax.axis_size(axis)
        return lax.ppermute(value, axis, [(i, i ^ (1 << number)) for i in range(size)])

    plans = [(0, tuple(range(1, bits))), (1, (0,) + tuple(range(2, bits)))]
    plan_of = [0] * (chunks - 1) + [1] if chunks > 1 else [0]
    order = sorted(range(chunks), key=lambda c: -plan_of[c])

    by_comp = strain.transpose(1, 0, 2)
    own = [by_comp[:, :, c * LANES : (c + 1) * LANES] for c in range(chunks)]
    info = dest[:, :, 0] * ROWS + det_row
    other = {c: swap(own[c], plans[plan_of[c]][0]) for c in order}
    used = sorted(set(plan_of))
    other_info = {k: swap(info, plans[k][0]) for k in used}
    own_list = {k: listing(info, me, *plans[k], angles, units) for k in used}
    other_list = {k: listing(other_info[k], me, *plans[k], angles, units) for k in used}

    weights = (dirs * SCALE).reshape(-1)
    rock = jnp.broadcast_to((rock_angles * SCALE)[:, None], (rocks, LANES))
    rock_index = lax.axis_index("rock").reshape(1)

    partial = {}
    for c in order:
        (partial[c],) = add_images(
            "own_images", own_list[plan_of[c]], weights, rock, own[c], None, [image_rows + rocks], 3_000_000
        )

    image = {}
    for c in order:
        k = plan_of[c]
        held = image_rows // 2
        sent, kept = add_images(
            "other_images", other_list[k], weights, rock, other[c], partial[c], [held, held], 3_000_000
        )
        for number in plans[k][1]:
            arrived = swap(sent, number)
            if held > unit:
                held = held // 2
                sent, kept = kept[:held] + arrived[:held], kept[held:] + arrived[held:]
            else:
                image[c] = kept + arrived

    def gather(value):
        parts = [value]
        for number in reversed(range(rock_size.bit_length() - 1)):
            parts = [x for part in parts for x in (part, swap(part, number, "rock"))]
        return parts

    groups = [order[:-1], order[-1:]]
    result = None
    for group in groups:
        value = jnp.concatenate([image[c] for c in group], axis=0) if len(group) > 1 else image[group[0]]
        result = resolve(rock_index, [c * LANES for c in group], pix, norm, result, resolution, gather(value))
    return result.reshape(angles, ROWS, rocks, pix)


def local(strain, dest, det_row, dirs, rock_angles, resolution):
    slabs = lax.axis_size("slab")
    rock_size = lax.axis_size("rock")
    tiles, unused, vox = strain.shape
    pix = resolution.shape[1]
    slots = slabs * (2 * tiles // slabs)
    images_smaller = slabs * ROWS * rock_angles.shape[0] * pix <= slots * dirs.shape[1] * vox
    powers = all(size & (size - 1) == 0 for size in (slabs, rock_size, tiles))
    regular = powers and slabs >= 4 and tiles % (2 * GROUP) == 0 and vox == pix and pix % LANES == 0
    plan = by_images if images_smaller and regular else by_tiles
    return plan(strain, dest, det_row, dirs, rock_angles, resolution)


def solution(mesh):
    placed = (
        P("slab", None, "rock"),
        P(None, "slab", None),
        P(None, "slab"),
        P(),
        P(),
        P(None, "rock"),
    )
    return jax.shard_map(
        local, mesh=mesh, in_specs=placed, out_specs=P(None, "slab", None, "rock"), check_vma=False
    )
```

```python
import math
import jax
import jax.numpy as jnp
from jax import lax
from jax.experimental import pallas as pl
from jax.experimental.pallas import tpu as pltpu
from jax.sharding import PartitionSpec as P

TILES_DEV = 128
DEPTH = 1
QDIR = 4
ROWS = 8
ANGLES = 2
LANES = 128
GROUP = 8
VMEM_LIMIT = 12 * 1024 * 1024
COST = 1024
SCHEDULE = (
    ("begin", 0),
    ("begin", 3),
    ("first", 0),
    ("first", 3),
    ("begin", 1),
    ("begin", 2),
    ("first", 1),
    ("middle", 0),
    ("rows", 0, 3, 1, 2),
    ("middle", 3),
    ("first", 2),
    ("middle", 1),
    ("final", 0),
    ("final", 3),
    ("middle", 2),
    ("final", 1),
    ("arrive", 0),
    ("arrive", 3),
    ("final", 2),
    ("near", 0, 3, 1, 2),
    ("arrive", 1),
    ("far", 0, 3, 1, 2),
    ("multiply", 0, 3, 1, 2),
)
SCALE = math.sqrt(0.5 / math.log(2.0))


def by_tiles(strain, dest, det_row, dirs, rock_angles, resolution):
    slabs = lax.axis_size("slab")
    tiles_here = strain.shape[0]
    vox_here = strain.shape[2]
    pix_here = resolution.shape[1]
    depth = vox_here // pix_here
    capacity = 2 * tiles_here // slabs
    slots = slabs * capacity
    block_size = 64
    rocks = rock_angles.shape[0]
    qcount = dirs.shape[1]
    norm = ROWS / (QDIR * DEPTH * TILES_DEV)
    row_ids = jnp.arange(ROWS, dtype=jnp.float32)
    lower = lax.broadcasted_iota(jnp.int32, (tiles_here, tiles_here), 1) < lax.broadcasted_iota(
        jnp.int32, (tiles_here, tiles_here), 0
    )

    def add_block(total, item):
        proj_block, row_block = item
        inten = jnp.sum(
            jnp.exp(-0.5 * (proj_block[:, :, None, :] - rock_angles[None, None, :, None]) ** 2),
            axis=1,
        )
        summed = inten.reshape(block_size, rocks, pix_here, depth).sum(axis=3)
        onehot = (row_ids[:, None] == row_block[None, :]).astype(jnp.float32)
        added = jnp.dot(
            onehot, summed.reshape(block_size, rocks * pix_here), precision=lax.Precision.HIGHEST
        )
        return (total + added, None)

    images = []
    for angle in range(ANGLES):
        owner = dest[angle, :, 0]
        same = (owner[:, None] == owner[None, :]) & lower
        rank = jnp.sum(same.astype(jnp.int32), axis=1)
        slot = owner * capacity + rank
        row_send = (
            jnp.full((slots,), -1.0, jnp.float32).at[slot].set(det_row[angle].astype(jnp.float32))
        )
        row_send = row_send.reshape(slabs, capacity)
        weights = dirs[angle]
        local_proj = jnp.einsum("qc,tcv->tqv", weights, strain, precision=lax.Precision.HIGHEST)
        outgoing = jnp.zeros((slots, qcount, vox_here), jnp.float32).at[slot].set(local_proj)
        outgoing = outgoing.reshape(slabs, capacity, qcount, vox_here)
        arrived, arrived_rows = (
            lax.all_to_all(outgoing, "slab", split_axis=0, concat_axis=0, tiled=True),
            lax.all_to_all(row_send, "slab", split_axis=0, concat_axis=0, tiled=True),
        )
        proj = arrived.reshape(slots, qcount, vox_here)
        proj_blocks = proj.reshape(slots // block_size, block_size, qcount, vox_here)
        row_blocks = arrived_rows.reshape(slots // block_size, block_size)
        image, unused = lax.scan(
            add_block, jnp.zeros((ROWS, rocks * pix_here), jnp.float32), (proj_blocks, row_blocks)
        )
        images.append(image.reshape(ROWS, rocks, pix_here) * norm)
    stacked = jnp.stack(images, axis=0)
    columns = resolution.astype(jnp.float32)
    return jnp.einsum(
        "agrp,pk->agrk",
        lax.all_gather(stacked, "rock", axis=3, tiled=True),
        columns,
        precision=lax.Precision.HIGHEST,
    )


def image_kernel(count_ref, list_ref, dirs_ref, rock_ref, strain_ref, *rest):
    proj = rest[-1]
    comps, tiles, pix = strain_ref.shape
    angles = count_ref.shape[0]
    qcount = dirs_ref.shape[1]
    rocks = rock_ref.shape[0]
    step = 4 * GROUP
    if len(rest) == 2:
        init, outs = None, rest[:1]
    else:
        init, outs = rest[0], rest[1:-2]
    acc = outs[0] if init is None else rest[-2]
    blocks = pix // LANES
    rows_out = acc.shape[0] // blocks
    row = lax.broadcasted_iota(jnp.int32, (rocks, LANES), 0)
    rock = jnp.zeros((rocks, LANES), jnp.float32)
    for i in range(rocks):
        rock = jnp.where(row == i, rock_ref[i] * SCALE, rock)
    if init is None:
        acc[...] = jnp.zeros_like(acc)
    else:
        acc[...] = init[...]

    for b in range(blocks):
        lanes = slice(b * LANES, (b + 1) * LANES)

        for k in range(angles * qcount):
            scaled = [dirs_ref[k // qcount, k % qcount, c] * SCALE for c in range(comps)]
            for start in range(0, tiles, step):
                rows = pl.ds(start, step)
                total = strain_ref[0, rows, lanes] * scaled[0]
                for c in range(1, comps):
                    total = total + strain_ref[c, rows, lanes] * scaled[c]
                proj[k, rows, :] = total

        for angle in range(angles):

            @pl.loop(0, (count_ref[angle] + GROUP - 1) // GROUP)
            def _(block):
                sums = []
                targets = []
                for j in range(GROUP):
                    code = list_ref[angle, block * GROUP + j]
                    tile = code & (tiles - 1)
                    target = (code >> (tiles - 1).bit_length()) * rocks
                    targets.append(pl.multiple_of(target + b * rows_out, rocks))
                    total = None
                    for q in range(qcount):
                        p = proj[angle * qcount + q, pl.ds(tile, 1), :]
                        d = jnp.broadcast_to(p, (rocks, LANES)) - rock
                        e = jnp.exp2(-(d * d))
                        total = e if total is None else total + e
                    sums.append(total)
                for target, total in zip(targets, sums):
                    acc[pl.ds(target, rocks), :] += total

    if init is not None:
        start = 0
        for out in outs:
            out[...] = acc[pl.ds(start, out.shape[0]), :]
            start += out.shape[0]


def add_images(name, listing, weights, rock, strain, init, sizes):
    counts, lists = listing
    comps, tiles, pix = strain.shape
    angles = counts.shape[0]
    qcount = weights.shape[1]
    smem = pl.BlockSpec(memory_space=pltpu.SMEM)
    vmem = pl.BlockSpec(memory_space=pltpu.VMEM)
    scratch = [pltpu.VMEM((angles * qcount, tiles, LANES), jnp.float32)]
    before = ()
    if init is not None:
        before = (init,)
        scratch = [pltpu.VMEM(init.shape, jnp.float32)] + scratch
    return pl.pallas_call(
        image_kernel,
        out_shape=tuple(jax.ShapeDtypeStruct((size, LANES), jnp.float32) for size in sizes),
        in_specs=[smem, smem, smem, smem] + [vmem] * (1 + len(before)),
        out_specs=tuple(vmem for size in sizes),
        scratch_shapes=scratch,
        compiler_params=pltpu.CompilerParams(vmem_limit_bytes=VMEM_LIMIT),
        cost_estimate=pl.CostEstimate(flops=COST, bytes_accessed=COST, transcendentals=0),
        name=name,
    )(counts, lists, weights, rock, strain, *before)


def resolve(norm, unit, total, blocks, parts):
    cols = blocks[0].shape[1]
    vmem = pl.BlockSpec(memory_space=pltpu.VMEM)
    before = () if total is None else (total,)

    def kernel(*refs):
        block_refs, part_refs, out_ref = refs[: len(blocks)], refs[len(blocks) : len(blocks) + len(parts)], refs[-1]
        values = [
            part[pl.ds(start, unit), :] * norm for part in part_refs for start in range(0, part.shape[0], unit)
        ]
        value = jnp.concatenate(values, axis=1)
        block = jnp.concatenate([ref[...] for ref in block_refs], axis=0)
        high = value.astype(jnp.bfloat16)
        low = (value - high.astype(jnp.float32)).astype(jnp.bfloat16)
        sums = jnp.dot(high, block, preferred_element_type=jnp.float32) + jnp.dot(
            low, block, preferred_element_type=jnp.float32
        )
        out_ref[...] = sums if total is None else sums + refs[-2][...]

    return pl.pallas_call(
        kernel,
        out_shape=jax.ShapeDtypeStruct((unit, cols), jnp.float32),
        in_specs=[vmem] * (len(blocks) + len(parts) + len(before)),
        out_specs=vmem,
        compiler_params=pltpu.CompilerParams(vmem_limit_bytes=VMEM_LIMIT),
        cost_estimate=pl.CostEstimate(flops=COST, bytes_accessed=COST, transcendentals=0),
        name="resolve",
    )(*blocks, *parts, *before)


def cut(by_comp):
    comps, tiles, pix = by_comp.shape
    count = pix // LANES

    def kernel(source, *rest):
        outs, sems = rest[:count], rest[count]
        copies = [
            pltpu.make_async_copy(source.at[:, :, pl.ds(c * LANES, LANES)], outs[c], sems.at[c]) for c in range(count)
        ]
        for copy in copies:
            copy.start()
        for copy in copies:
            copy.wait()

    return pl.pallas_call(
        kernel,
        out_shape=[jax.ShapeDtypeStruct((comps, tiles, LANES), jnp.float32)] * count,
        in_specs=[pl.BlockSpec(memory_space=pl.ANY)],
        out_specs=[pl.BlockSpec(memory_space=pltpu.VMEM)] * count,
        scratch_shapes=[pltpu.SemaphoreType.DMA((count,))],
        compiler_params=pltpu.CompilerParams(vmem_limit_bytes=VMEM_LIMIT),
        cost_estimate=pl.CostEstimate(flops=COST, bytes_accessed=COST, transcendentals=0),
        name="cut",
    )(by_comp)


def bit(value, number):
    return (value >> number) & 1


def listing(info, me, raw, halves, angles, units):
    tiles = info.shape[1]
    owner = info // ROWS
    keep = bit(owner, raw) == bit(me, raw)
    position = jnp.zeros_like(owner)
    for number in halves:
        position = 2 * position + (bit(owner, number) == bit(me, number)).astype(jnp.int32)
    target = (position * angles + jnp.arange(angles)[:, None]) * ROWS + info % ROWS
    number = jnp.arange(tiles)
    earlier = keep[:, None, :] & (number[None, None, :] < number[None, :, None])
    rank = jnp.where(keep, jnp.sum(earlier.astype(jnp.int32), axis=2), -1)
    code = number[None, :] + tiles * (target - units)
    lists = tiles * units + jnp.sum(
        jnp.where(rank[:, None, :] == number[None, :, None], code[:, None, :], 0), axis=2
    )
    return jnp.sum(keep.astype(jnp.int32), axis=1), lists


def by_images(strain, dest, det_row, dirs, rock_angles, resolution):
    slabs = lax.axis_size("slab")
    rock_size = lax.axis_size("rock")
    tiles = strain.shape[0]
    pix = resolution.shape[1]
    rocks = rock_angles.shape[0]
    angles, qcount, comps = dirs.shape
    norm = ROWS / (QDIR * DEPTH * TILES_DEV)
    bits = slabs.bit_length() - 1
    unit = angles * ROWS * rocks
    units = slabs // 2 * angles * ROWS
    image_rows = units * rocks
    me = lax.axis_index("slab")
    chunks = pix // LANES

    def swap(value, number, axis="slab"):
        size = lax.axis_size(axis)
        return lax.ppermute(value, axis, [(i, i ^ (1 << number)) for i in range(size)])

    plans = [(0, tuple(range(1, bits))), (1, tuple(range(2, bits)) + (0,))]
    plan_of = [0] * (chunks - 1) + [1] if chunks > 1 else [0]
    early = [c for c in range(chunks) if plan_of[c] == 0]
    late = [c for c in range(chunks) if plan_of[c] == 1]
    last = []

    def tie(value):
        return lax.optimization_barrier((value, *last))[0]

    def mark(value):
        last[:] = [value]
        return value

    own = cut(strain.transpose(1, 0, 2))
    other = {c: swap(own[c], plans[plan_of[c]][0]) for c in early[:1] + late + early[1:]}
    mark(own[0])
    info = tie(dest[:, :, 0] * ROWS + det_row)
    used = sorted(set(plan_of))
    other_info = {k: swap(info, plans[k][0]) for k in used}
    own_list = {k: listing(info, me, *plans[k], angles, units) for k in used}
    other_list = {k: listing(other_info[k], me, *plans[k], angles, units) for k in used}


    partial = {}
    held = {}
    flying = {}
    half = image_rows // 2

    def begin(c):
        (partial[c],) = add_images(
            "own_images",
            own_list[plan_of[c]],
            dirs,
            rock_angles,
            tie(own[c]),
            None,
            [image_rows + rocks],
        )
        mark(partial[c])

    def first(c):
        k = plan_of[c]
        sent, held[c] = add_images(
            "other_images", other_list[k], dirs, rock_angles, tie(other[c]), partial[c], [half, half]
        )
        mark(sent)
        flying[c] = swap(sent, plans[k][1][0])

    def middle(c):
        arrived = tie(flying[c])
        for number in plans[plan_of[c]][1][1:]:
            rows = held[c].shape[0] // 2
            sent = mark(held[c][:rows] + arrived[:rows])
            flying[c] = swap(sent, number)
            held[c] = held[c][rows:] + arrived[rows:]
            arrived = flying[c]

    lower = list(reversed(range(max(rock_size.bit_length() - 2, 0))))
    image = {}
    beside = {}

    def spread(part):
        found = [part]
        for number in lower:
            found = [x for p in found for x in (p, swap(p, number, "rock"))]
        return found

    def final(c):
        image[c] = mark(held[c] + tie(flying[c]))
        if rock_size > 1:
            beside[c] = swap(image[c], len(lower), "rock")

    def arrive(c):
        if rock_size > 1:
            beside[c] = mark(tie(beside[c]))

    def join(values):
        return jnp.concatenate(values, axis=0) if len(values) > 1 else values[0]

    rock_index = lax.axis_index("rock")
    found = {}
    blocks = {}
    result = []

    def near(*group):
        found[group] = spread(mark(join([image[c] for c in group])))

    def far(*group):
        if rock_size > 1:
            found[group] = found[group] + spread(mark(tie(join([beside[c] for c in group]))))

    def rows(*group):
        source = tie(resolution)
        places = [(rock_index ^ j) * pix + c * LANES for j in range(rock_size) for c in group]
        blocks[group] = [lax.dynamic_slice(source, (at, 0), (LANES, resolution.shape[1])) for at in places]
        mark(blocks[group][-1])

    def multiply(*group):
        parts = found[group]
        total = result[-1] if result else None
        result.append(mark(resolve(norm, unit, total, blocks[group], [tie(parts[0])] + parts[1:])))

    if (len(early), len(late)) == (3, 1):
        steps = SCHEDULE
    else:
        every = early + late
        steps = [(name, c) for name in ("begin", "first", "middle", "final") for c in every]
        steps += [("rows", *every), ("near", *every), ("far", *every), ("multiply", *every)]
    doing = dict(begin=begin, first=first, middle=middle, final=final, arrive=arrive, near=near, far=far, rows=rows)
    doing["multiply"] = multiply
    for name, *group in steps:
        doing[name](*group)
    return result[-1].reshape(angles, ROWS, rocks, pix)


def local(strain, dest, det_row, dirs, rock_angles, resolution):
    slabs = lax.axis_size("slab")
    rock_size = lax.axis_size("rock")
    tiles, unused, vox = strain.shape
    pix = resolution.shape[1]
    slots = slabs * (2 * tiles // slabs)
    images_smaller = slabs * ROWS * rock_angles.shape[0] * pix <= slots * dirs.shape[1] * vox
    powers = all(size & (size - 1) == 0 for size in (slabs, rock_size, tiles))
    regular = powers and slabs >= 4 and tiles % (4 * GROUP) == 0 and vox == pix and pix % LANES == 0
    plan = by_images if images_smaller and regular else by_tiles
    return plan(strain, dest, det_row, dirs, rock_angles, resolution)


def solution(mesh):
    placed = (
        P("slab", None, "rock"),
        P(None, "slab", None),
        P(None, "slab"),
        P(),
        P(),
        P(None, "rock"),
    )
    return jax.shard_map(
        local, mesh=mesh, in_specs=placed, out_specs=P(None, "slab", None, "rock"), check_vma=False
    )
```

```python
import math
import jax
import jax.numpy as jnp
from jax import lax
from jax.experimental import pallas as pl
from jax.experimental.pallas import tpu as pltpu
from jax.sharding import PartitionSpec as P

TILES_DEV = 128
DEPTH = 1
QDIR = 4
ROWS = 8
ANGLES = 2
LANES = 128
GROUP = 8
VMEM_LIMIT = 12 * 1024 * 1024
COST = 1024
SCHEDULE = (
    ("begin", 0, 1),
    ("first", 0),
    ("first", 1),
    ("begin", 2, 3),
    ("middle", 0),
    ("first", 2),
    ("rows", 0, 1),
    ("rows", 2, 3),
    ("middle", 1),
    ("first", 3),
    ("final", 0),
    ("middle", 2),
    ("final", 1),
    ("arrive", 0),
    ("middle", 3),
    ("final", 2),
    ("arrive", 1),
    ("near", 0, 1),
    ("far", 0, 1),
    ("final", 3),
    ("multiply", 0, 1),
    ("near", 2, 3),
    ("arrive", 2),
    ("far", 2, 3),
    ("multiply", 2, 3),
)
SCHEDULED = (1, 1, 1, 1)
SCALE = math.sqrt(0.5 / math.log(2.0))


def by_tiles(strain, dest, det_row, dirs, rock_angles, resolution):
    slabs = lax.axis_size("slab")
    tiles_here = strain.shape[0]
    vox_here = strain.shape[2]
    pix_here = resolution.shape[1]
    depth = vox_here // pix_here
    capacity = 2 * tiles_here // slabs
    slots = slabs * capacity
    block_size = 64
    rocks = rock_angles.shape[0]
    qcount = dirs.shape[1]
    norm = ROWS / (QDIR * DEPTH * TILES_DEV)
    row_ids = jnp.arange(ROWS, dtype=jnp.float32)
    lower = lax.broadcasted_iota(jnp.int32, (tiles_here, tiles_here), 1) < lax.broadcasted_iota(
        jnp.int32, (tiles_here, tiles_here), 0
    )

    def add_block(total, item):
        proj_block, row_block = item
        inten = jnp.sum(
            jnp.exp(-0.5 * (proj_block[:, :, None, :] - rock_angles[None, None, :, None]) ** 2),
            axis=1,
        )
        summed = inten.reshape(block_size, rocks, pix_here, depth).sum(axis=3)
        onehot = (row_ids[:, None] == row_block[None, :]).astype(jnp.float32)
        added = jnp.dot(
            onehot, summed.reshape(block_size, rocks * pix_here), precision=lax.Precision.HIGHEST
        )
        return (total + added, None)

    images = []
    for angle in range(ANGLES):
        owner = dest[angle, :, 0]
        same = (owner[:, None] == owner[None, :]) & lower
        rank = jnp.sum(same.astype(jnp.int32), axis=1)
        slot = owner * capacity + rank
        row_send = (
            jnp.full((slots,), -1.0, jnp.float32).at[slot].set(det_row[angle].astype(jnp.float32))
        )
        row_send = row_send.reshape(slabs, capacity)
        weights = dirs[angle]
        local_proj = jnp.einsum("qc,tcv->tqv", weights, strain, precision=lax.Precision.HIGHEST)
        outgoing = jnp.zeros((slots, qcount, vox_here), jnp.float32).at[slot].set(local_proj)
        outgoing = outgoing.reshape(slabs, capacity, qcount, vox_here)
        arrived, arrived_rows = (
            lax.all_to_all(outgoing, "slab", split_axis=0, concat_axis=0, tiled=True),
            lax.all_to_all(row_send, "slab", split_axis=0, concat_axis=0, tiled=True),
        )
        proj = arrived.reshape(slots, qcount, vox_here)
        proj_blocks = proj.reshape(slots // block_size, block_size, qcount, vox_here)
        row_blocks = arrived_rows.reshape(slots // block_size, block_size)
        image, unused = lax.scan(
            add_block, jnp.zeros((ROWS, rocks * pix_here), jnp.float32), (proj_blocks, row_blocks)
        )
        images.append(image.reshape(ROWS, rocks, pix_here) * norm)
    stacked = jnp.stack(images, axis=0)
    columns = resolution.astype(jnp.float32)
    return jnp.einsum(
        "agrp,pk->agrk",
        lax.all_gather(stacked, "rock", axis=3, tiled=True),
        columns,
        precision=lax.Precision.HIGHEST,
    )


def prepared_rocks(rock_ref):
    rocks = rock_ref.shape[0]
    row = lax.broadcasted_iota(jnp.int32, (rocks, LANES), 0)
    rock = jnp.zeros((rocks, LANES), jnp.float32)
    for i in range(rocks):
        rock = jnp.where(row == i, rock_ref[i] * SCALE, rock)
    return rock


def add_tiles(count_ref, list_ref, dirs_ref, rock, strain_ref, proj, acc):
    angles, qcount, comps = dirs_ref.shape
    tiles, lanes = proj.shape[1:]
    rocks = rock.shape[0]
    step = 4 * GROUP
    twice = rock + rock
    for k in range(angles * qcount):
        scaled = [dirs_ref[k // qcount, k % qcount, c] * SCALE for c in range(comps)]
        for start in range(0, tiles, step):
            total = None
            for c in range(comps):
                part = strain_ref[pl.ds((c * tiles + start) // GROUP, step // GROUP)] * scaled[c]
                total = part if total is None else total + part
            proj[k, pl.ds(start, step), :] = total.reshape(step, lanes)

    for angle in range(angles):

        @pl.loop(0, (count_ref[angle] + GROUP - 1) // GROUP)
        def _(block):
            sums = []
            targets = []
            for j in range(GROUP):
                code = list_ref[angle, block * GROUP + j]
                tile = code & (tiles - 1)
                target = (code >> (tiles - 1).bit_length()) * rocks
                targets.append(pl.multiple_of(target, rocks))
                total = None
                for q in range(qcount):
                    p = jnp.broadcast_to(proj[angle * qcount + q, pl.ds(tile, 1), :], (rocks, lanes))
                    e = jnp.exp2(p * (twice - p))
                    total = e if total is None else total + e
                sums.append(total)
            for target, total in zip(targets, sums):
                acc[pl.ds(target, rocks), :] += total


def own_images(plan_of, listings, dirs, rock, strains, tiles, rows):
    used = len(listings)
    count = len(strains)
    angles, qcount, comps = dirs.shape

    def kernel(*refs):
        list_refs = refs[: 2 * used]
        dirs_ref, rock_ref = refs[2 * used : 2 * used + 2]
        strain_refs = refs[2 * used + 2 : 2 * used + 2 + count]
        outs, proj = refs[-1 - count : -1], refs[-1]
        rock = prepared_rocks(rock_ref)
        for c in range(count):
            k = plan_of[c]
            outs[c][...] = jnp.zeros_like(outs[c])
            add_tiles(list_refs[2 * k], list_refs[2 * k + 1], dirs_ref, rock, strain_refs[c], proj, outs[c])

    smem = pl.BlockSpec(memory_space=pltpu.SMEM)
    vmem = pl.BlockSpec(memory_space=pltpu.VMEM)
    return pl.pallas_call(
        kernel,
        out_shape=[jax.ShapeDtypeStruct((rows, LANES), jnp.float32)] * count,
        in_specs=[smem] * (2 * used + 2) + [vmem] * count,
        out_specs=[vmem] * count,
        scratch_shapes=[pltpu.VMEM((angles * qcount, tiles, LANES), jnp.float32)],
        compiler_params=pltpu.CompilerParams(vmem_limit_bytes=VMEM_LIMIT // 2),
        cost_estimate=pl.CostEstimate(flops=COST, bytes_accessed=COST, transcendentals=0),
        name="own_images",
    )(*[x for listing in listings for x in listing], dirs, rock, *strains)


def other_images(listing, dirs, rock, strain, init, tiles, half):
    angles, qcount, comps = dirs.shape
    rocks = rock.shape[0]

    def kernel(count_ref, list_ref, dirs_ref, rock_ref, strain_ref, init_ref, sent_ref, kept_ref, acc, proj):
        rock = prepared_rocks(rock_ref)
        acc[...] = init_ref[...]
        add_tiles(count_ref, list_ref, dirs_ref, rock, strain_ref, proj, acc)
        factor = jnp.exp2(-(rock * rock))
        for start, out in ((0, sent_ref), (half, kept_ref)):
            for row in range(0, half, rocks):
                out[pl.ds(row, rocks), :] = acc[pl.ds(start + row, rocks), :] * factor

    smem = pl.BlockSpec(memory_space=pltpu.SMEM)
    vmem = pl.BlockSpec(memory_space=pltpu.VMEM)
    return pl.pallas_call(
        kernel,
        out_shape=[jax.ShapeDtypeStruct((half, LANES), jnp.float32)] * 2,
        in_specs=[smem] * 4 + [vmem] * 2,
        out_specs=[vmem] * 2,
        scratch_shapes=[
            pltpu.VMEM(init.shape, jnp.float32),
            pltpu.VMEM((angles * qcount, tiles, LANES), jnp.float32),
        ],
        compiler_params=pltpu.CompilerParams(vmem_limit_bytes=VMEM_LIMIT // 4),
        cost_estimate=pl.CostEstimate(flops=COST, bytes_accessed=COST, transcendentals=0),
        name="other_images",
    )(*listing, dirs, rock, strain, init)


def resolve(norm, unit, total, blocks, parts):
    cols = blocks[0].shape[1]
    vmem = pl.BlockSpec(memory_space=pltpu.VMEM)
    before = () if total is None else (total,)

    def kernel(*refs):
        block_refs, part_refs, out_ref = refs[: len(blocks)], refs[len(blocks) : len(blocks) + len(parts)], refs[-1]
        values = [
            part[pl.ds(start, unit), :] * norm for part in part_refs for start in range(0, part.shape[0], unit)
        ]
        value = jnp.concatenate(values, axis=1)
        block = jnp.concatenate([ref[...] for ref in block_refs], axis=0)
        high = value.astype(jnp.bfloat16)
        low = (value - high.astype(jnp.float32)).astype(jnp.bfloat16)
        sums = jnp.dot(high, block, preferred_element_type=jnp.float32) + jnp.dot(
            low, block, preferred_element_type=jnp.float32
        )
        out_ref[...] = sums if total is None else sums + refs[-2][...]

    return pl.pallas_call(
        kernel,
        out_shape=jax.ShapeDtypeStruct((unit, cols), jnp.float32),
        in_specs=[vmem] * (len(blocks) + len(parts) + len(before)),
        out_specs=vmem,
        compiler_params=pltpu.CompilerParams(vmem_limit_bytes=VMEM_LIMIT),
        cost_estimate=pl.CostEstimate(flops=COST, bytes_accessed=COST, transcendentals=0),
        name="resolve",
    )(*blocks, *parts, *before)


def bit(value, number):
    return (value >> number) & 1


def listing(info, me, raw, halves, angles, units):
    tiles = info.shape[1]
    owner = info // ROWS
    keep = bit(owner, raw) == bit(me, raw)
    position = jnp.zeros_like(owner)
    for number in halves:
        position = 2 * position + (bit(owner, number) == bit(me, number)).astype(jnp.int32)
    target = (position * angles + jnp.arange(angles)[:, None]) * ROWS + info % ROWS
    number = jnp.arange(tiles)
    earlier = keep[:, None, :] & (number[None, None, :] < number[None, :, None])
    rank = jnp.where(keep, jnp.sum(earlier.astype(jnp.int32), axis=2), -1)
    code = number[None, :] + tiles * (target - units)
    lists = tiles * units + jnp.sum(
        jnp.where(rank[:, None, :] == number[None, :, None], code[:, None, :], 0), axis=2
    )
    return jnp.sum(keep.astype(jnp.int32), axis=1), lists


def by_images(strain, dest, det_row, dirs, rock_angles, resolution):
    slabs = lax.axis_size("slab")
    rock_size = lax.axis_size("rock")
    tiles = strain.shape[0]
    pix = resolution.shape[1]
    rocks = rock_angles.shape[0]
    angles, qcount, comps = dirs.shape
    norm = ROWS / (QDIR * DEPTH * TILES_DEV)
    bits = slabs.bit_length() - 1
    unit = angles * ROWS * rocks
    units = slabs // 2 * angles * ROWS
    image_rows = units * rocks
    me = lax.axis_index("slab")
    chunks = pix // LANES

    odd = lax.axis_index("rock") & 1

    def swap(value, number, axis="slab"):
        if axis == "slab" and number[0] != number[1]:
            pairs = [
                (i * rock_size + j, (i ^ (1 << number[j & 1])) * rock_size + j)
                for i in range(slabs)
                for j in range(rock_size)
            ]
            return lax.ppermute(value, ("slab", "rock"), pairs)
        number = number[0] if axis == "slab" else number
        return lax.ppermute(value, axis, [(i, i ^ (1 << number)) for i in range(lax.axis_size(axis))])

    same = [(k, k) for k in range(bits)]
    plans = [(same[0], tuple(same[1:])), ((1, 0), ((0, 1),) + tuple(same[2:]))]
    plan_of = [1] * chunks
    every = list(range(chunks))
    launches = every
    last = []

    def tie(value):
        return lax.optimization_barrier((value, *last))[0]

    def mark(value):
        last[:] = [value]
        return value

    info = dest[:, :, 0] * ROWS + det_row
    info_rows = angles * tiles // LANES
    padded = jnp.pad(info.astype(jnp.float32).reshape(info_rows, LANES), ((0, -info_rows % GROUP), (0, 0)))
    by_comp = strain.transpose(1, 0, 2).reshape(comps * tiles // GROUP, GROUP, pix)
    padded = padded.reshape(-1, GROUP, LANES)
    own = {}
    other = {}
    told = []
    source = by_comp
    for c in launches:
        block = source[:, :, c * LANES : (c + 1) * LANES]
        if plan_of[c] not in told:
            told.append(plan_of[c])
            block = jnp.concatenate([block, padded], axis=0)
        own[c] = block
        other[c] = swap(block, plans[plan_of[c]][0])
        if c == launches[0]:
            mark(block)
            source = tie(by_comp)
    mark(own[launches[-1]])
    used = sorted(set(plan_of))

    def numbers(k):
        raw, halves = plans[k]
        pick = lambda pair: pair[0] if pair[0] == pair[1] else jnp.where(odd == 1, pair[1], pair[0])
        return pick(raw), [pick(pair) for pair in halves]

    own_list = {k: listing(tie(info), me, *numbers(k), angles, units) for k in used}
    other_list = {}

    def learn(c):
        arrived = mark(tie(other[c]))
        below = arrived[by_comp.shape[0] :].reshape(-1, LANES)[:info_rows]
        below = below.reshape(angles, tiles).astype(jnp.int32)
        other_list[plan_of[c]] = listing(below, me, *numbers(plan_of[c]), angles, units)

    partial = {}
    held = {}
    flying = {}
    half = image_rows // 2

    def begin(*group):
        kinds = sorted({plan_of[c] for c in group})
        found = own_images(
            [kinds.index(plan_of[c]) for c in group],
            [own_list[k] for k in kinds],
            dirs,
            rock_angles,
            [tie(own[group[0]])] + [own[c] for c in group[1:]],
            tiles,
            image_rows + rocks,
        )
        partial.update(zip(group, found))
        mark(found[0])

    def first(c):
        k = plan_of[c]
        if k not in other_list:
            learn(c)
        sent, held[c] = other_images(other_list[k], dirs, rock_angles, tie(other[c]), partial[c], tiles, half)
        mark(sent)
        flying[c] = swap(sent, plans[k][1][0])

    def middle(c):
        arrived = tie(flying[c])
        for number in plans[plan_of[c]][1][1:]:
            rows = held[c].shape[0] // 2
            sent = mark(held[c][:rows] + arrived[:rows])
            flying[c] = swap(sent, number)
            held[c] = held[c][rows:] + arrived[rows:]
            arrived = flying[c]

    lower = list(reversed(range(max(rock_size.bit_length() - 2, 0))))
    image = {}
    beside = {}

    def spread(part):
        found = [part]
        for number in lower:
            found = [x for p in found for x in (p, swap(p, number, "rock"))]
        return found

    def final(c):
        image[c] = mark(held[c] + tie(flying[c]))
        if rock_size > 1:
            beside[c] = swap(image[c], len(lower), "rock")

    def arrive(c):
        if rock_size > 1:
            beside[c] = mark(tie(beside[c]))

    def join(values):
        return jnp.concatenate(values, axis=0) if len(values) > 1 else values[0]

    rock_index = lax.axis_index("rock")
    found = {}
    blocks = {}
    result = []

    def near(*group):
        found[group] = spread(mark(join([image[c] for c in group])))

    def far(*group):
        if rock_size > 1:
            found[group] = found[group] + spread(mark(tie(join([beside[c] for c in group]))))

    def rows(*group):
        source = tie(resolution)
        places = [(rock_index ^ j) * pix + c * LANES for j in range(rock_size) for c in group]
        blocks[group] = [lax.dynamic_slice(source, (at, 0), (LANES, resolution.shape[1])) for at in places]
        mark(blocks[group][-1])

    def multiply(*group):
        parts = found[group]
        total = result[-1] if result else None
        result.append(mark(resolve(norm, unit, total, blocks[group], [tie(parts[0])] + parts[1:])))

    if plan_of == list(SCHEDULED):
        steps = SCHEDULE
    else:
        steps = [("begin", *every)] + [(name, c) for name in ("first", "middle", "final") for c in every]
        steps += [("rows", *every), ("near", *every), ("far", *every), ("multiply", *every)]
    doing = dict(begin=begin, first=first, middle=middle, final=final, arrive=arrive, near=near, far=far, rows=rows)
    doing["multiply"] = multiply
    for name, *group in steps:
        doing[name](*group)
    return result[-1].reshape(angles, ROWS, rocks, pix)


def local(strain, dest, det_row, dirs, rock_angles, resolution):
    slabs = lax.axis_size("slab")
    rock_size = lax.axis_size("rock")
    tiles, unused, vox = strain.shape
    pix = resolution.shape[1]
    slots = slabs * (2 * tiles // slabs)
    images_smaller = slabs * ROWS * rock_angles.shape[0] * pix <= slots * dirs.shape[1] * vox
    powers = all(size & (size - 1) == 0 for size in (slabs, rock_size, tiles))
    regular = powers and slabs >= 4 and tiles % LANES == 0 and vox == pix and pix % LANES == 0
    plan = by_images if images_smaller and regular else by_tiles
    return plan(strain, dest, det_row, dirs, rock_angles, resolution)


def solution(mesh):
    placed = (
        P("slab", None, "rock"),
        P(None, "slab", None),
        P(None, "slab"),
        P(),
        P(),
        P(None, "rock"),
    )
    return jax.shard_map(
        local, mesh=mesh, in_specs=placed, out_specs=P(None, "slab", None, "rock"), check_vma=False
    )
```

```python
import math
import jax
import jax.numpy as jnp
from jax import lax
from jax.experimental import pallas as pl
from jax.experimental.pallas import tpu as pltpu
from jax.sharding import PartitionSpec as P

TILES_DEV = 128
DEPTH = 1
QDIR = 4
ROWS = 8
ANGLES = 2
LANES = 128
GROUP = 8
VMEM_LIMIT = 12 * 1024 * 1024
COST = 1024
SCHEDULE = (
    ("begin", 0, 1),
    ("launch", 2),
    ("first", 0),
    ("first", 1),
    ("launch", 3),
    ("begin", 2, 3),
    ("middle", 0),
    ("first", 2),
    ("rows", 0, 1),
    ("rows", 2, 3),
    ("middle", 1),
    ("first", 3),
    ("middle", 2),
    ("final", 0),
    ("final", 1),
    ("arrive", 0),
    ("middle", 3),
    ("final", 2),
    ("arrive", 1),
    ("near", 0, 1),
    ("far", 0, 1),
    ("final", 3),
    ("multiply", 0, 1),
    ("near", 2, 3),
    ("arrive", 2),
    ("far", 2, 3),
    ("multiply", 2, 3),
)
SCHEDULED = (1, 1, 1, 0)
SCALE = math.sqrt(0.5 / math.log(2.0))


def by_tiles(strain, dest, det_row, dirs, rock_angles, resolution):
    slabs = lax.axis_size("slab")
    tiles_here = strain.shape[0]
    vox_here = strain.shape[2]
    pix_here = resolution.shape[1]
    depth = vox_here // pix_here
    capacity = 2 * tiles_here // slabs
    slots = slabs * capacity
    block_size = 64
    rocks = rock_angles.shape[0]
    qcount = dirs.shape[1]
    norm = ROWS / (QDIR * DEPTH * TILES_DEV)
    row_ids = jnp.arange(ROWS, dtype=jnp.float32)
    lower = lax.broadcasted_iota(jnp.int32, (tiles_here, tiles_here), 1) < lax.broadcasted_iota(
        jnp.int32, (tiles_here, tiles_here), 0
    )

    def add_block(total, item):
        proj_block, row_block = item
        inten = jnp.sum(
            jnp.exp(-0.5 * (proj_block[:, :, None, :] - rock_angles[None, None, :, None]) ** 2),
            axis=1,
        )
        summed = inten.reshape(block_size, rocks, pix_here, depth).sum(axis=3)
        onehot = (row_ids[:, None] == row_block[None, :]).astype(jnp.float32)
        added = jnp.dot(
            onehot, summed.reshape(block_size, rocks * pix_here), precision=lax.Precision.HIGHEST
        )
        return (total + added, None)

    images = []
    for angle in range(ANGLES):
        owner = dest[angle, :, 0]
        same = (owner[:, None] == owner[None, :]) & lower
        rank = jnp.sum(same.astype(jnp.int32), axis=1)
        slot = owner * capacity + rank
        row_send = (
            jnp.full((slots,), -1.0, jnp.float32).at[slot].set(det_row[angle].astype(jnp.float32))
        )
        row_send = row_send.reshape(slabs, capacity)
        weights = dirs[angle]
        local_proj = jnp.einsum("qc,tcv->tqv", weights, strain, precision=lax.Precision.HIGHEST)
        outgoing = jnp.zeros((slots, qcount, vox_here), jnp.float32).at[slot].set(local_proj)
        outgoing = outgoing.reshape(slabs, capacity, qcount, vox_here)
        arrived, arrived_rows = (
            lax.all_to_all(outgoing, "slab", split_axis=0, concat_axis=0, tiled=True),
            lax.all_to_all(row_send, "slab", split_axis=0, concat_axis=0, tiled=True),
        )
        proj = arrived.reshape(slots, qcount, vox_here)
        proj_blocks = proj.reshape(slots // block_size, block_size, qcount, vox_here)
        row_blocks = arrived_rows.reshape(slots // block_size, block_size)
        image, unused = lax.scan(
            add_block, jnp.zeros((ROWS, rocks * pix_here), jnp.float32), (proj_blocks, row_blocks)
        )
        images.append(image.reshape(ROWS, rocks, pix_here) * norm)
    stacked = jnp.stack(images, axis=0)
    columns = resolution.astype(jnp.float32)
    return jnp.einsum(
        "agrp,pk->agrk",
        lax.all_gather(stacked, "rock", axis=3, tiled=True),
        columns,
        precision=lax.Precision.HIGHEST,
    )


def prepared_rocks(rock_ref):
    rocks = rock_ref.shape[0]
    row = lax.broadcasted_iota(jnp.int32, (rocks, LANES), 0)
    rock = jnp.zeros((rocks, LANES), jnp.float32)
    for i in range(rocks):
        rock = jnp.where(row == i, rock_ref[i] * SCALE, rock)
    return rock


def add_tiles(count_ref, list_ref, dirs_ref, rock, strain_ref, proj, acc):
    angles, qcount, comps = dirs_ref.shape
    tiles, lanes = proj.shape[1:]
    rocks = rock.shape[0]
    step = 4 * GROUP
    twice = rock + rock
    for k in range(angles * qcount):
        scaled = [dirs_ref[k // qcount, k % qcount, c] * SCALE for c in range(comps)]
        for start in range(0, tiles, step):
            total = None
            for c in range(comps):
                part = strain_ref[pl.ds((c * tiles + start) // GROUP, step // GROUP)] * scaled[c]
                total = part if total is None else total + part
            proj[k, pl.ds(start, step), :] = total.reshape(step, lanes)

    for angle in range(angles):

        @pl.loop(0, (count_ref[angle] + GROUP - 1) // GROUP)
        def _(block):
            sums = []
            targets = []
            for j in range(GROUP):
                code = list_ref[angle, block * GROUP + j]
                tile = code & (tiles - 1)
                target = (code >> (tiles - 1).bit_length()) * rocks
                targets.append(pl.multiple_of(target, rocks))
                total = None
                for q in range(qcount):
                    p = jnp.broadcast_to(proj[angle * qcount + q, pl.ds(tile, 1), :], (rocks, lanes))
                    e = jnp.exp2(p * (twice - p))
                    total = e if total is None else total + e
                sums.append(total)
            for target, total in zip(targets, sums):
                acc[pl.ds(target, rocks), :] += total


def own_images(plan_of, listings, dirs, rock, strains, tiles, rows):
    used = len(listings)
    count = len(strains)
    angles, qcount, comps = dirs.shape

    def kernel(*refs):
        list_refs = refs[: 2 * used]
        dirs_ref, rock_ref = refs[2 * used : 2 * used + 2]
        strain_refs = refs[2 * used + 2 : 2 * used + 2 + count]
        outs, proj = refs[-1 - count : -1], refs[-1]
        rock = prepared_rocks(rock_ref)
        for c in range(count):
            k = plan_of[c]
            outs[c][...] = jnp.zeros_like(outs[c])
            add_tiles(list_refs[2 * k], list_refs[2 * k + 1], dirs_ref, rock, strain_refs[c], proj, outs[c])

    smem = pl.BlockSpec(memory_space=pltpu.SMEM)
    vmem = pl.BlockSpec(memory_space=pltpu.VMEM)
    return pl.pallas_call(
        kernel,
        out_shape=[jax.ShapeDtypeStruct((rows, LANES), jnp.float32)] * count,
        in_specs=[smem] * (2 * used + 2) + [vmem] * count,
        out_specs=[vmem] * count,
        scratch_shapes=[pltpu.VMEM((angles * qcount, tiles, LANES), jnp.float32)],
        compiler_params=pltpu.CompilerParams(vmem_limit_bytes=VMEM_LIMIT // 2),
        cost_estimate=pl.CostEstimate(flops=COST, bytes_accessed=COST, transcendentals=0),
        name="own_images",
    )(*[x for listing in listings for x in listing], dirs, rock, *strains)


def other_images(listing, dirs, rock, strain, init, tiles, half):
    angles, qcount, comps = dirs.shape
    rocks = rock.shape[0]

    def kernel(count_ref, list_ref, dirs_ref, rock_ref, strain_ref, init_ref, sent_ref, kept_ref, acc, proj):
        rock = prepared_rocks(rock_ref)
        acc[...] = init_ref[...]
        add_tiles(count_ref, list_ref, dirs_ref, rock, strain_ref, proj, acc)
        factor = jnp.exp2(-(rock * rock))
        for start, out in ((0, sent_ref), (half, kept_ref)):
            for row in range(0, half, rocks):
                out[pl.ds(row, rocks), :] = acc[pl.ds(start + row, rocks), :] * factor

    smem = pl.BlockSpec(memory_space=pltpu.SMEM)
    vmem = pl.BlockSpec(memory_space=pltpu.VMEM)
    return pl.pallas_call(
        kernel,
        out_shape=[jax.ShapeDtypeStruct((half, LANES), jnp.float32)] * 2,
        in_specs=[smem] * 4 + [vmem] * 2,
        out_specs=[vmem] * 2,
        scratch_shapes=[
            pltpu.VMEM(init.shape, jnp.float32),
            pltpu.VMEM((angles * qcount, tiles, LANES), jnp.float32),
        ],
        compiler_params=pltpu.CompilerParams(vmem_limit_bytes=VMEM_LIMIT // 4),
        cost_estimate=pl.CostEstimate(flops=COST, bytes_accessed=COST, transcendentals=0),
        name="other_images",
    )(*listing, dirs, rock, strain, init)


def resolve(norm, unit, total, blocks, parts):
    cols = blocks[0].shape[1]
    vmem = pl.BlockSpec(memory_space=pltpu.VMEM)
    before = () if total is None else (total,)

    def kernel(*refs):
        block_refs, part_refs, out_ref = refs[: len(blocks)], refs[len(blocks) : len(blocks) + len(parts)], refs[-1]
        values = [
            part[pl.ds(start, unit), :] * norm for part in part_refs for start in range(0, part.shape[0], unit)
        ]
        value = jnp.concatenate(values, axis=1)
        block = jnp.concatenate([ref[...] for ref in block_refs], axis=0)
        high = value.astype(jnp.bfloat16)
        low = (value - high.astype(jnp.float32)).astype(jnp.bfloat16)
        sums = jnp.dot(high, block, preferred_element_type=jnp.float32) + jnp.dot(
            low, block, preferred_element_type=jnp.float32
        )
        out_ref[...] = sums if total is None else sums + refs[-2][...]

    return pl.pallas_call(
        kernel,
        out_shape=jax.ShapeDtypeStruct((unit, cols), jnp.float32),
        in_specs=[vmem] * (len(blocks) + len(parts) + len(before)),
        out_specs=vmem,
        compiler_params=pltpu.CompilerParams(vmem_limit_bytes=VMEM_LIMIT),
        cost_estimate=pl.CostEstimate(flops=COST, bytes_accessed=COST, transcendentals=0),
        name="resolve",
    )(*blocks, *parts, *before)


def bit(value, number):
    return (value >> number) & 1


def listing(info, me, raw, halves, angles, units):
    tiles = info.shape[1]
    owner = info // ROWS
    keep = bit(owner, raw) == bit(me, raw)
    position = jnp.zeros_like(owner)
    for number in halves:
        position = 2 * position + (bit(owner, number) == bit(me, number)).astype(jnp.int32)
    target = (position * angles + jnp.arange(angles)[:, None]) * ROWS + info % ROWS
    number = jnp.arange(tiles)
    earlier = keep[:, None, :] & (number[None, None, :] < number[None, :, None])
    rank = jnp.where(keep, jnp.sum(earlier.astype(jnp.int32), axis=2), -1)
    code = number[None, :] + tiles * (target - units)
    lists = tiles * units + jnp.sum(
        jnp.where(rank[:, None, :] == number[None, :, None], code[:, None, :], 0), axis=2
    )
    return jnp.sum(keep.astype(jnp.int32), axis=1), lists


def by_images(strain, dest, det_row, dirs, rock_angles, resolution):
    slabs = lax.axis_size("slab")
    rock_size = lax.axis_size("rock")
    tiles = strain.shape[0]
    pix = resolution.shape[1]
    rocks = rock_angles.shape[0]
    angles, qcount, comps = dirs.shape
    norm = ROWS / (QDIR * DEPTH * TILES_DEV)
    bits = slabs.bit_length() - 1
    unit = angles * ROWS * rocks
    units = slabs // 2 * angles * ROWS
    image_rows = units * rocks
    me = lax.axis_index("slab")
    chunks = pix // LANES

    odd = lax.axis_index("rock") & 1

    def swap(value, number, axis="slab"):
        if axis == "slab" and number[0] != number[1]:
            pairs = [
                (i * rock_size + j, (i ^ (1 << number[j & 1])) * rock_size + j)
                for i in range(slabs)
                for j in range(rock_size)
            ]
            return lax.ppermute(value, ("slab", "rock"), pairs)
        number = number[0] if axis == "slab" else number
        return lax.ppermute(value, axis, [(i, i ^ (1 << number)) for i in range(lax.axis_size(axis))])

    same = [(k, k) for k in range(bits)]
    plans = [(same[0], tuple(same[1:])), ((1, 0), ((0, 1),) + tuple(same[2:]))]
    plan_of = [1] * (chunks - 1) + [0]
    every = list(range(chunks))
    launches = every
    last = []

    def tie(value):
        return lax.optimization_barrier((value, *last))[0]

    def mark(value):
        last[:] = [value]
        return value

    info = dest[:, :, 0] * ROWS + det_row
    info_rows = angles * tiles // LANES
    padded = jnp.pad(info.astype(jnp.float32).reshape(info_rows, LANES), ((0, -info_rows % GROUP), (0, 0)))
    by_comp = strain.transpose(1, 0, 2).reshape(comps * tiles // GROUP, GROUP, pix)
    padded = padded.reshape(-1, GROUP, LANES)
    own = {}
    other = {}

    def piece(source, c):
        block = source[:, :, c * LANES : (c + 1) * LANES]
        if plan_of[c] in plan_of[:c]:
            return block
        return jnp.concatenate([block, padded], axis=0)

    def launch(c):
        own[c] = mark(tie(pieces[c]) if last else pieces[c])
        other[c] = swap(own[c], plans[plan_of[c]][0])

    pieces = {0: piece(by_comp, 0)}
    launch(0)
    source = tie(by_comp)
    pieces.update({c: piece(source, c) for c in every[1:]})
    if chunks > 1:
        launch(1)
    used = sorted(set(plan_of))

    def numbers(k):
        raw, halves = plans[k]
        pick = lambda pair: pair[0] if pair[0] == pair[1] else jnp.where(odd == 1, pair[1], pair[0])
        return pick(raw), [pick(pair) for pair in halves]

    own_list = {k: listing(tie(info), me, *numbers(k), angles, units) for k in used}
    other_list = {}

    def learn(c):
        arrived = mark(tie(other[c]))
        below = arrived[by_comp.shape[0] :].reshape(-1, LANES)[:info_rows]
        below = below.reshape(angles, tiles).astype(jnp.int32)
        other_list[plan_of[c]] = listing(below, me, *numbers(plan_of[c]), angles, units)

    partial = {}
    held = {}
    flying = {}
    half = image_rows // 2

    def begin(*group):
        kinds = sorted({plan_of[c] for c in group})
        found = own_images(
            [kinds.index(plan_of[c]) for c in group],
            [own_list[k] for k in kinds],
            dirs,
            rock_angles,
            [tie(own[group[0]])] + [own[c] for c in group[1:]],
            tiles,
            image_rows + rocks,
        )
        partial.update(zip(group, found))
        mark(found[0])

    def first(c):
        k = plan_of[c]
        if k not in other_list:
            learn(c)
        sent, held[c] = other_images(other_list[k], dirs, rock_angles, tie(other[c]), partial[c], tiles, half)
        mark(sent)
        flying[c] = swap(sent, plans[k][1][0])

    def middle(c):
        arrived = tie(flying[c])
        for number in plans[plan_of[c]][1][1:]:
            rows = held[c].shape[0] // 2
            sent = mark(held[c][:rows] + arrived[:rows])
            flying[c] = swap(sent, number)
            held[c] = held[c][rows:] + arrived[rows:]
            arrived = flying[c]

    lower = list(reversed(range(max(rock_size.bit_length() - 2, 0))))
    image = {}
    beside = {}

    def spread(part):
        found = [part]
        for number in lower:
            found = [x for p in found for x in (p, swap(p, number, "rock"))]
        return found

    def final(c):
        image[c] = mark(held[c] + tie(flying[c]))
        if rock_size > 1:
            beside[c] = swap(image[c], len(lower), "rock")

    def arrive(c):
        if rock_size > 1:
            beside[c] = mark(tie(beside[c]))

    def join(values):
        return jnp.concatenate(values, axis=0) if len(values) > 1 else values[0]

    rock_index = lax.axis_index("rock")
    found = {}
    blocks = {}
    result = []

    def near(*group):
        found[group] = spread(mark(join([image[c] for c in group])))

    def far(*group):
        if rock_size > 1:
            found[group] = found[group] + spread(mark(tie(join([beside[c] for c in group]))))

    def rows(*group):
        source = tie(resolution)
        places = [(rock_index ^ j) * pix + c * LANES for j in range(rock_size) for c in group]
        blocks[group] = [lax.dynamic_slice(source, (at, 0), (LANES, resolution.shape[1])) for at in places]
        mark(blocks[group][-1])

    def multiply(*group):
        parts = found[group]
        total = result[-1] if result else None
        result.append(mark(resolve(norm, unit, total, blocks[group], [tie(parts[0])] + parts[1:])))

    if plan_of == list(SCHEDULED):
        steps = SCHEDULE
    else:
        steps = [("launch", c) for c in every[2:]] + [("begin", *every)] + [(name, c) for name in ("first", "middle", "final") for c in every]
        steps += [("rows", *every), ("near", *every), ("far", *every), ("multiply", *every)]
    doing = dict(begin=begin, first=first, middle=middle, final=final, arrive=arrive, near=near, far=far, rows=rows)
    doing["multiply"] = multiply
    doing["launch"] = launch
    doing["wait"] = lambda c: other.update({c: mark(tie(other[c]))})
    for name, *group in steps:
        doing[name](*group)
    return result[-1].reshape(angles, ROWS, rocks, pix)


def local(strain, dest, det_row, dirs, rock_angles, resolution):
    slabs = lax.axis_size("slab")
    rock_size = lax.axis_size("rock")
    tiles, unused, vox = strain.shape
    pix = resolution.shape[1]
    slots = slabs * (2 * tiles // slabs)
    images_smaller = slabs * ROWS * rock_angles.shape[0] * pix <= slots * dirs.shape[1] * vox
    powers = all(size & (size - 1) == 0 for size in (slabs, rock_size, tiles))
    regular = powers and slabs >= 4 and tiles % LANES == 0 and vox == pix and pix % LANES == 0
    plan = by_images if images_smaller and regular else by_tiles
    return plan(strain, dest, det_row, dirs, rock_angles, resolution)


def solution(mesh):
    placed = (
        P("slab", None, "rock"),
        P(None, "slab", None),
        P(None, "slab"),
        P(),
        P(),
        P(None, "rock"),
    )
    return jax.shard_map(
        local, mesh=mesh, in_specs=placed, out_specs=P(None, "slab", None, "rock"), check_vma=False
    )
```

```python
import math
import jax
import jax.numpy as jnp
from jax import lax
from jax.experimental import pallas as pl
from jax.experimental.pallas import tpu as pltpu
from jax.sharding import PartitionSpec as P

TILES_DEV = 128
DEPTH = 1
QDIR = 4
ROWS = 8
ANGLES = 2
LANES = 128
GROUP = 8
VMEM_LIMIT = 12 * 1024 * 1024
COST = 1024
SCHEDULE = (
    ("begin", 0, 1),
    ("launch", 2),
    ("first", 0),
    ("first", 1),
    ("launch", 3),
    ("begin", 2, 3),
    ("middle", 0),
    ("first", 2),
    ("rows", 0, 1),
    ("rows", 2, 3),
    ("middle", 1),
    ("first", 3),
    ("final", 0),
    ("middle", 2),
    ("final", 1),
    ("arrive", 0),
    ("middle", 3),
    ("final", 2),
    ("arrive", 1),
    ("final", 3),
    ("near", 0, 1),
    ("far", 0, 1),
    ("multiply", 0, 1),
    ("near", 2, 3),
    ("arrive", 2),
    ("far", 2, 3),
    ("multiply", 2, 3),
)
SCHEDULED = (1, 1, 1, 0)
SCALE = math.sqrt(0.5 / math.log(2.0))


def by_tiles(strain, dest, det_row, dirs, rock_angles, resolution):
    slabs = lax.axis_size("slab")
    tiles_here = strain.shape[0]
    vox_here = strain.shape[2]
    pix_here = resolution.shape[1]
    depth = vox_here // pix_here
    capacity = 2 * tiles_here // slabs
    slots = slabs * capacity
    block_size = 64
    rocks = rock_angles.shape[0]
    qcount = dirs.shape[1]
    norm = ROWS / (QDIR * DEPTH * TILES_DEV)
    row_ids = jnp.arange(ROWS, dtype=jnp.float32)
    lower = lax.broadcasted_iota(jnp.int32, (tiles_here, tiles_here), 1) < lax.broadcasted_iota(
        jnp.int32, (tiles_here, tiles_here), 0
    )

    def add_block(total, item):
        proj_block, row_block = item
        inten = jnp.sum(
            jnp.exp(-0.5 * (proj_block[:, :, None, :] - rock_angles[None, None, :, None]) ** 2),
            axis=1,
        )
        summed = inten.reshape(block_size, rocks, pix_here, depth).sum(axis=3)
        onehot = (row_ids[:, None] == row_block[None, :]).astype(jnp.float32)
        added = jnp.dot(
            onehot, summed.reshape(block_size, rocks * pix_here), precision=lax.Precision.HIGHEST
        )
        return (total + added, None)

    images = []
    for angle in range(ANGLES):
        owner = dest[angle, :, 0]
        same = (owner[:, None] == owner[None, :]) & lower
        rank = jnp.sum(same.astype(jnp.int32), axis=1)
        slot = owner * capacity + rank
        row_send = (
            jnp.full((slots,), -1.0, jnp.float32).at[slot].set(det_row[angle].astype(jnp.float32))
        )
        row_send = row_send.reshape(slabs, capacity)
        weights = dirs[angle]
        local_proj = jnp.einsum("qc,tcv->tqv", weights, strain, precision=lax.Precision.HIGHEST)
        outgoing = jnp.zeros((slots, qcount, vox_here), jnp.float32).at[slot].set(local_proj)
        outgoing = outgoing.reshape(slabs, capacity, qcount, vox_here)
        arrived, arrived_rows = (
            lax.all_to_all(outgoing, "slab", split_axis=0, concat_axis=0, tiled=True),
            lax.all_to_all(row_send, "slab", split_axis=0, concat_axis=0, tiled=True),
        )
        proj = arrived.reshape(slots, qcount, vox_here)
        proj_blocks = proj.reshape(slots // block_size, block_size, qcount, vox_here)
        row_blocks = arrived_rows.reshape(slots // block_size, block_size)
        image, unused = lax.scan(
            add_block, jnp.zeros((ROWS, rocks * pix_here), jnp.float32), (proj_blocks, row_blocks)
        )
        images.append(image.reshape(ROWS, rocks, pix_here) * norm)
    stacked = jnp.stack(images, axis=0)
    columns = resolution.astype(jnp.float32)
    return jnp.einsum(
        "agrp,pk->agrk",
        lax.all_gather(stacked, "rock", axis=3, tiled=True),
        columns,
        precision=lax.Precision.HIGHEST,
    )


def prepared_rocks(rock_ref):
    rocks = rock_ref.shape[0]
    row = lax.broadcasted_iota(jnp.int32, (rocks, LANES), 0)
    rock = jnp.zeros((rocks, LANES), jnp.float32)
    for i in range(rocks):
        rock = jnp.where(row == i, rock_ref[i] * SCALE, rock)
    return rock


def add_tiles(count_ref, list_ref, dirs_ref, rock, strain_ref, proj, acc):
    angles, qcount, comps = dirs_ref.shape
    tiles, lanes = proj.shape[1:]
    rocks = rock.shape[0]
    step = 4 * GROUP
    twice = rock + rock
    for k in range(angles * qcount):
        scaled = [dirs_ref[k // qcount, k % qcount, c] * SCALE for c in range(comps)]
        for start in range(0, tiles, step):
            total = None
            for c in range(comps):
                part = strain_ref[pl.ds((c * tiles + start) // GROUP, step // GROUP)] * scaled[c]
                total = part if total is None else total + part
            proj[k, pl.ds(start, step), :] = total.reshape(step, lanes)

    for angle in range(angles):

        @pl.loop(0, (count_ref[angle] + GROUP - 1) // GROUP)
        def _(block):
            sums = []
            targets = []
            for j in range(GROUP):
                code = list_ref[angle, block * GROUP + j]
                tile = code & (tiles - 1)
                target = (code >> (tiles - 1).bit_length()) * rocks
                targets.append(pl.multiple_of(target, rocks))
                total = None
                for q in range(qcount):
                    p = jnp.broadcast_to(proj[angle * qcount + q, pl.ds(tile, 1), :], (rocks, lanes))
                    e = jnp.exp2(p * (twice - p))
                    total = e if total is None else total + e
                sums.append(total)
            for target, total in zip(targets, sums):
                acc[pl.ds(target, rocks), :] += total


def own_images(plan_of, listings, dirs, rock, strains, tiles, rows):
    used = len(listings)
    count = len(strains)
    angles, qcount, comps = dirs.shape

    def kernel(*refs):
        list_refs = refs[: 2 * used]
        dirs_ref, rock_ref = refs[2 * used : 2 * used + 2]
        strain_refs = refs[2 * used + 2 : 2 * used + 2 + count]
        outs, proj = refs[-1 - count : -1], refs[-1]
        rock = prepared_rocks(rock_ref)
        for c in range(count):
            k = plan_of[c]
            outs[c][...] = jnp.zeros_like(outs[c])
            add_tiles(list_refs[2 * k], list_refs[2 * k + 1], dirs_ref, rock, strain_refs[c], proj, outs[c])

    smem = pl.BlockSpec(memory_space=pltpu.SMEM)
    vmem = pl.BlockSpec(memory_space=pltpu.VMEM)
    return pl.pallas_call(
        kernel,
        out_shape=[jax.ShapeDtypeStruct((rows, LANES), jnp.float32)] * count,
        in_specs=[smem] * (2 * used + 2) + [vmem] * count,
        out_specs=[vmem] * count,
        scratch_shapes=[pltpu.VMEM((angles * qcount, tiles, LANES), jnp.float32)],
        compiler_params=pltpu.CompilerParams(vmem_limit_bytes=VMEM_LIMIT // 2),
        cost_estimate=pl.CostEstimate(flops=COST, bytes_accessed=COST, transcendentals=0),
        name="own_images",
    )(*[x for listing in listings for x in listing], dirs, rock, *strains)


def other_images(listing, dirs, rock, strain, init, tiles, half):
    angles, qcount, comps = dirs.shape
    rocks = rock.shape[0]

    def kernel(count_ref, list_ref, dirs_ref, rock_ref, strain_ref, init_ref, sent_ref, kept_ref, acc, proj):
        rock = prepared_rocks(rock_ref)
        acc[...] = init_ref[...]
        add_tiles(count_ref, list_ref, dirs_ref, rock, strain_ref, proj, acc)
        factor = jnp.exp2(-(rock * rock))
        for start, out in ((0, sent_ref), (half, kept_ref)):
            for row in range(0, half, rocks):
                out[pl.ds(row, rocks), :] = acc[pl.ds(start + row, rocks), :] * factor

    smem = pl.BlockSpec(memory_space=pltpu.SMEM)
    vmem = pl.BlockSpec(memory_space=pltpu.VMEM)
    return pl.pallas_call(
        kernel,
        out_shape=[jax.ShapeDtypeStruct((half, LANES), jnp.float32)] * 2,
        in_specs=[smem] * 4 + [vmem] * 2,
        out_specs=[vmem] * 2,
        scratch_shapes=[
            pltpu.VMEM(init.shape, jnp.float32),
            pltpu.VMEM((angles * qcount, tiles, LANES), jnp.float32),
        ],
        compiler_params=pltpu.CompilerParams(vmem_limit_bytes=VMEM_LIMIT // 4),
        cost_estimate=pl.CostEstimate(flops=COST, bytes_accessed=COST, transcendentals=0),
        name="other_images",
    )(*listing, dirs, rock, strain, init)


def resolve(norm, unit, total, blocks, parts):
    cols = blocks[0].shape[1]
    vmem = pl.BlockSpec(memory_space=pltpu.VMEM)
    before = () if total is None else (total,)

    def kernel(*refs):
        block_refs, part_refs, out_ref = refs[: len(blocks)], refs[len(blocks) : len(blocks) + len(parts)], refs[-1]
        values = [
            part[pl.ds(start, unit), :] * norm for part in part_refs for start in range(0, part.shape[0], unit)
        ]
        value = jnp.concatenate(values, axis=1)
        block = jnp.concatenate([ref[...] for ref in block_refs], axis=0)
        high = value.astype(jnp.bfloat16)
        low = (value - high.astype(jnp.float32)).astype(jnp.bfloat16)
        sums = jnp.dot(high, block, preferred_element_type=jnp.float32) + jnp.dot(
            low, block, preferred_element_type=jnp.float32
        )
        out_ref[...] = sums if total is None else sums + refs[-2][...]

    return pl.pallas_call(
        kernel,
        out_shape=jax.ShapeDtypeStruct((unit, cols), jnp.float32),
        in_specs=[vmem] * (len(blocks) + len(parts) + len(before)),
        out_specs=vmem,
        compiler_params=pltpu.CompilerParams(vmem_limit_bytes=VMEM_LIMIT),
        cost_estimate=pl.CostEstimate(flops=COST, bytes_accessed=COST, transcendentals=0),
        name="resolve",
    )(*blocks, *parts, *before)


def bit(value, number):
    return (value >> number) & 1


def listing(info, me, raw, halves, angles, units):
    tiles = info.shape[1]
    owner = info // ROWS
    keep = bit(owner, raw) == bit(me, raw)
    position = jnp.zeros_like(owner)
    for number in halves:
        position = 2 * position + (bit(owner, number) == bit(me, number)).astype(jnp.int32)
    target = (position * angles + jnp.arange(angles)[:, None]) * ROWS + info % ROWS
    number = jnp.arange(tiles)
    earlier = keep[:, None, :] & (number[None, None, :] < number[None, :, None])
    rank = jnp.where(keep, jnp.sum(earlier.astype(jnp.int32), axis=2), -1)
    code = number[None, :] + tiles * (target - units)
    lists = tiles * units + jnp.sum(
        jnp.where(rank[:, None, :] == number[None, :, None], code[:, None, :], 0), axis=2
    )
    return jnp.sum(keep.astype(jnp.int32), axis=1), lists


def by_images(strain, dest, det_row, dirs, rock_angles, resolution):
    slabs = lax.axis_size("slab")
    rock_size = lax.axis_size("rock")
    tiles = strain.shape[0]
    pix = resolution.shape[1]
    rocks = rock_angles.shape[0]
    angles, qcount, comps = dirs.shape
    norm = ROWS / (QDIR * DEPTH * TILES_DEV)
    bits = slabs.bit_length() - 1
    unit = angles * ROWS * rocks
    units = slabs // 2 * angles * ROWS
    image_rows = units * rocks
    me = lax.axis_index("slab")
    chunks = pix // LANES

    odd = lax.axis_index("rock") & 1

    def swap(value, number, axis="slab"):
        if axis == "slab" and number[0] != number[1]:
            pairs = [
                (i * rock_size + j, (i ^ (1 << number[j & 1])) * rock_size + j)
                for i in range(slabs)
                for j in range(rock_size)
            ]
            return lax.ppermute(value, ("slab", "rock"), pairs)
        number = number[0] if axis == "slab" else number
        return lax.ppermute(value, axis, [(i, i ^ (1 << number)) for i in range(lax.axis_size(axis))])

    same = [(k, k) for k in range(bits)]
    plans = [(same[0], tuple(same[1:])), ((1, 0), ((0, 1),) + tuple(same[2:]))]
    plan_of = [1] * (chunks - 1) + [0]
    every = list(range(chunks))
    launches = every
    last = []

    def tie(value):
        return lax.optimization_barrier((value, *last))[0]

    def mark(value):
        last[:] = [value]
        return value

    info = dest[:, :, 0] * ROWS + det_row
    info_rows = angles * tiles // LANES
    padded = jnp.pad(info.astype(jnp.float32).reshape(info_rows, LANES), ((0, -info_rows % GROUP), (0, 0)))
    by_comp = strain.transpose(1, 0, 2).reshape(comps * tiles // GROUP, GROUP, pix)
    padded = padded.reshape(-1, GROUP, LANES)
    own = {}
    other = {}

    def piece(source, c):
        block = source[:, :, c * LANES : (c + 1) * LANES]
        if plan_of[c] in plan_of[:c]:
            return block
        return jnp.concatenate([block, padded], axis=0)

    def launch(c):
        own[c] = mark(tie(pieces[c]) if last else pieces[c])
        other[c] = swap(own[c], plans[plan_of[c]][0])

    pieces = {0: piece(by_comp, 0)}
    launch(0)
    source = tie(by_comp)
    pieces.update({c: piece(source, c) for c in every[1:]})
    if chunks > 1:
        launch(1)
    used = sorted(set(plan_of))

    def numbers(k):
        raw, halves = plans[k]
        pick = lambda pair: pair[0] if pair[0] == pair[1] else jnp.where(odd == 1, pair[1], pair[0])
        return pick(raw), [pick(pair) for pair in halves]

    own_list = {k: listing(tie(info), me, *numbers(k), angles, units) for k in used}
    other_list = {}

    def learn(c):
        arrived = mark(tie(other[c]))
        below = arrived[by_comp.shape[0] :].reshape(-1, LANES)[:info_rows]
        below = below.reshape(angles, tiles).astype(jnp.int32)
        other_list[plan_of[c]] = listing(below, me, *numbers(plan_of[c]), angles, units)

    partial = {}
    held = {}
    flying = {}
    half = image_rows // 2

    def begin(*group):
        kinds = sorted({plan_of[c] for c in group})
        found = own_images(
            [kinds.index(plan_of[c]) for c in group],
            [own_list[k] for k in kinds],
            dirs,
            rock_angles,
            [tie(own[group[0]])] + [own[c] for c in group[1:]],
            tiles,
            image_rows + rocks,
        )
        partial.update(zip(group, found))
        mark(found[0])

    def first(c):
        k = plan_of[c]
        if k not in other_list:
            learn(c)
        sent, held[c] = other_images(other_list[k], dirs, rock_angles, tie(other[c]), partial[c], tiles, half)
        mark(sent)
        flying[c] = swap(sent, plans[k][1][0])

    def middle(c):
        arrived = tie(flying[c])
        for number in plans[plan_of[c]][1][1:]:
            rows = held[c].shape[0] // 2
            sent = mark(held[c][:rows] + arrived[:rows])
            flying[c] = swap(sent, number)
            held[c] = held[c][rows:] + arrived[rows:]
            arrived = flying[c]

    lower = list(reversed(range(max(rock_size.bit_length() - 2, 0))))
    image = {}
    beside = {}

    def spread(part):
        found = [part]
        for number in lower:
            found = [x for p in found for x in (p, swap(p, number, "rock"))]
        return found

    def final(c):
        image[c] = mark(held[c] + tie(flying[c]))
        if rock_size > 1:
            beside[c] = swap(image[c], len(lower), "rock")

    def arrive(c):
        if rock_size > 1:
            beside[c] = mark(tie(beside[c]))

    def join(values):
        return jnp.concatenate(values, axis=0) if len(values) > 1 else values[0]

    rock_index = lax.axis_index("rock")
    found = {}
    blocks = {}
    result = []

    def near(*group):
        found[group] = spread(mark(join([image[c] for c in group])))

    def far(*group):
        if rock_size > 1:
            found[group] = found[group] + spread(mark(tie(join([beside[c] for c in group]))))

    def rows(*group):
        source = tie(resolution)
        places = [(rock_index ^ j) * pix + c * LANES for j in range(rock_size) for c in group]
        blocks[group] = [lax.dynamic_slice(source, (at, 0), (LANES, resolution.shape[1])) for at in places]
        mark(blocks[group][-1])

    def multiply(*group):
        parts = found[group]
        total = result[-1] if result else None
        result.append(mark(resolve(norm, unit, total, blocks[group], [tie(parts[0])] + parts[1:])))

    if plan_of == list(SCHEDULED):
        steps = SCHEDULE
    else:
        steps = [("launch", c) for c in every[2:]] + [("begin", *every)] + [(name, c) for name in ("first", "middle", "final") for c in every]
        steps += [("rows", *every), ("near", *every), ("far", *every), ("multiply", *every)]
    doing = dict(begin=begin, first=first, middle=middle, final=final, arrive=arrive, near=near, far=far, rows=rows)
    doing["multiply"] = multiply
    doing["launch"] = launch
    doing["wait"] = lambda c: other.update({c: mark(tie(other[c]))})
    for name, *group in steps:
        doing[name](*group)
    return result[-1].reshape(angles, ROWS, rocks, pix)


def local(strain, dest, det_row, dirs, rock_angles, resolution):
    slabs = lax.axis_size("slab")
    rock_size = lax.axis_size("rock")
    tiles, unused, vox = strain.shape
    pix = resolution.shape[1]
    slots = slabs * (2 * tiles // slabs)
    images_smaller = slabs * ROWS * rock_angles.shape[0] * pix <= slots * dirs.shape[1] * vox
    powers = all(size & (size - 1) == 0 for size in (slabs, rock_size, tiles))
    regular = powers and slabs >= 4 and tiles % LANES == 0 and vox == pix and pix % LANES == 0
    plan = by_images if images_smaller and regular else by_tiles
    return plan(strain, dest, det_row, dirs, rock_angles, resolution)


def solution(mesh):
    placed = (
        P("slab", None, "rock"),
        P(None, "slab", None),
        P(None, "slab"),
        P(),
        P(),
        P(None, "rock"),
    )
    return jax.shard_map(
        local, mesh=mesh, in_specs=placed, out_specs=P(None, "slab", None, "rock"), check_vma=False
    )
```

```python
import math
import jax
import jax.numpy as jnp
from jax import lax
from jax.experimental import pallas as pl
from jax.experimental.pallas import tpu as pltpu
from jax.sharding import PartitionSpec as P

TILES_DEV = 128
DEPTH = 1
QDIR = 4
ROWS = 8
ANGLES = 2
LANES = 128
GROUP = 8
VMEM_LIMIT = 12 * 1024 * 1024
COST = 1024
SCHEDULE = (
    ("begin", 0, 1),
    ("launch", 2),
    ("first", 0),
    ("first", 1),
    ("launch", 3),
    ("begin", 2, 3),
    ("middle", 0),
    ("first", 2),
    ("rows", 0, 1),
    ("rows", 2, 3),
    ("middle", 1),
    ("first", 3),
    ("final", 0),
    ("middle", 2),
    ("final", 1),
    ("arrive", 0),
    ("middle", 3),
    ("final", 2),
    ("arrive", 1),
    ("final", 3),
    ("near", 0, 1),
    ("far", 0, 1),
    ("multiply", 0, 1),
    ("near", 2, 3),
    ("arrive", 2),
    ("far", 2, 3),
    ("multiply", 2, 3),
)
SCHEDULED = (1, 1, 1, 0)
SCALE = math.sqrt(0.5 / math.log(2.0))


def by_tiles(strain, dest, det_row, dirs, rock_angles, resolution):
    slabs = lax.axis_size("slab")
    tiles_here = strain.shape[0]
    vox_here = strain.shape[2]
    pix_here = resolution.shape[1]
    depth = vox_here // pix_here
    capacity = 2 * tiles_here // slabs
    slots = slabs * capacity
    block_size = 64
    rocks = rock_angles.shape[0]
    qcount = dirs.shape[1]
    norm = ROWS / (QDIR * DEPTH * TILES_DEV)
    row_ids = jnp.arange(ROWS, dtype=jnp.float32)
    lower = lax.broadcasted_iota(jnp.int32, (tiles_here, tiles_here), 1) < lax.broadcasted_iota(
        jnp.int32, (tiles_here, tiles_here), 0
    )

    def add_block(total, item):
        proj_block, row_block = item
        inten = jnp.sum(
            jnp.exp(-0.5 * (proj_block[:, :, None, :] - rock_angles[None, None, :, None]) ** 2),
            axis=1,
        )
        summed = inten.reshape(block_size, rocks, pix_here, depth).sum(axis=3)
        onehot = (row_ids[:, None] == row_block[None, :]).astype(jnp.float32)
        added = jnp.dot(
            onehot, summed.reshape(block_size, rocks * pix_here), precision=lax.Precision.HIGHEST
        )
        return (total + added, None)

    images = []
    for angle in range(ANGLES):
        owner = dest[angle, :, 0]
        same = (owner[:, None] == owner[None, :]) & lower
        rank = jnp.sum(same.astype(jnp.int32), axis=1)
        slot = owner * capacity + rank
        row_send = (
            jnp.full((slots,), -1.0, jnp.float32).at[slot].set(det_row[angle].astype(jnp.float32))
        )
        row_send = row_send.reshape(slabs, capacity)
        weights = dirs[angle]
        local_proj = jnp.einsum("qc,tcv->tqv", weights, strain, precision=lax.Precision.HIGHEST)
        outgoing = jnp.zeros((slots, qcount, vox_here), jnp.float32).at[slot].set(local_proj)
        outgoing = outgoing.reshape(slabs, capacity, qcount, vox_here)
        arrived, arrived_rows = (
            lax.all_to_all(outgoing, "slab", split_axis=0, concat_axis=0, tiled=True),
            lax.all_to_all(row_send, "slab", split_axis=0, concat_axis=0, tiled=True),
        )
        proj = arrived.reshape(slots, qcount, vox_here)
        proj_blocks = proj.reshape(slots // block_size, block_size, qcount, vox_here)
        row_blocks = arrived_rows.reshape(slots // block_size, block_size)
        image, unused = lax.scan(
            add_block, jnp.zeros((ROWS, rocks * pix_here), jnp.float32), (proj_blocks, row_blocks)
        )
        images.append(image.reshape(ROWS, rocks, pix_here) * norm)
    stacked = jnp.stack(images, axis=0)
    columns = resolution.astype(jnp.float32)
    return jnp.einsum(
        "agrp,pk->agrk",
        lax.all_gather(stacked, "rock", axis=3, tiled=True),
        columns,
        precision=lax.Precision.HIGHEST,
    )


def prepared_rocks(rock_ref):
    rocks = rock_ref.shape[0]
    row = lax.broadcasted_iota(jnp.int32, (rocks, LANES), 0)
    rock = jnp.zeros((rocks, LANES), jnp.float32)
    for i in range(rocks):
        rock = jnp.where(row == i, rock_ref[i] * SCALE, rock)
    return rock


def add_tiles(count_ref, list_ref, dirs_ref, rock, strain_ref, proj, acc):
    angles, qcount, comps = dirs_ref.shape
    tiles, lanes = proj.shape[1:]
    rocks = rock.shape[0]
    step = 4 * GROUP
    twice = rock + rock
    for k in range(angles * qcount):
        scaled = [dirs_ref[k // qcount, k % qcount, c] * SCALE for c in range(comps)]
        for start in range(0, tiles, step):
            total = None
            for c in range(comps):
                part = strain_ref[pl.ds((c * tiles + start) // GROUP, step // GROUP)] * scaled[c]
                total = part if total is None else total + part
            proj[k, pl.ds(start, step), :] = total.reshape(step, lanes)

    for angle in range(angles):

        @pl.loop(0, (count_ref[angle] + GROUP - 1) // GROUP)
        def _(block):
            sums = []
            targets = []
            for j in range(GROUP):
                code = list_ref[angle, block * GROUP + j]
                tile = code & (tiles - 1)
                target = (code >> (tiles - 1).bit_length()) * rocks
                targets.append(pl.multiple_of(target, rocks))
                total = None
                for q in range(qcount):
                    p = jnp.broadcast_to(proj[angle * qcount + q, pl.ds(tile, 1), :], (rocks, lanes))
                    e = jnp.exp2(p * (twice - p))
                    total = e if total is None else total + e
                sums.append(total)
            for target, total in zip(targets, sums):
                acc[pl.ds(target, rocks), :] += total


def own_images(plan_of, listings, dirs, rock, strains, tiles, rows):
    used = len(listings)
    count = len(strains)
    angles, qcount, comps = dirs.shape

    def kernel(*refs):
        list_refs = refs[: 2 * used]
        dirs_ref, rock_ref = refs[2 * used : 2 * used + 2]
        strain_refs = refs[2 * used + 2 : 2 * used + 2 + count]
        outs, proj = refs[-1 - count : -1], refs[-1]
        rock = prepared_rocks(rock_ref)
        for c in range(count):
            k = plan_of[c]
            outs[c][...] = jnp.zeros_like(outs[c])
            add_tiles(list_refs[2 * k], list_refs[2 * k + 1], dirs_ref, rock, strain_refs[c], proj, outs[c])

    smem = pl.BlockSpec(memory_space=pltpu.SMEM)
    vmem = pl.BlockSpec(memory_space=pltpu.VMEM)
    return pl.pallas_call(
        kernel,
        out_shape=[jax.ShapeDtypeStruct((rows, LANES), jnp.float32)] * count,
        in_specs=[smem] * (2 * used + 2) + [vmem] * count,
        out_specs=[vmem] * count,
        scratch_shapes=[pltpu.VMEM((angles * qcount, tiles, LANES), jnp.float32)],
        compiler_params=pltpu.CompilerParams(vmem_limit_bytes=VMEM_LIMIT // 2),
        cost_estimate=pl.CostEstimate(flops=COST, bytes_accessed=COST, transcendentals=0),
        name="own_images",
    )(*[x for listing in listings for x in listing], dirs, rock, *strains)


def other_images(listing, dirs, rock, strain, init, tiles, half, norm):
    angles, qcount, comps = dirs.shape
    rocks = rock.shape[0]

    def kernel(count_ref, list_ref, dirs_ref, rock_ref, strain_ref, init_ref, sent_ref, kept_ref, acc, proj):
        rock = prepared_rocks(rock_ref)
        acc[...] = init_ref[...]
        add_tiles(count_ref, list_ref, dirs_ref, rock, strain_ref, proj, acc)
        factor = jnp.exp2(-(rock * rock)) * norm
        for start, out in ((0, sent_ref), (half, kept_ref)):
            for row in range(0, half, rocks):
                out[pl.ds(row, rocks), :] = acc[pl.ds(start + row, rocks), :] * factor

    smem = pl.BlockSpec(memory_space=pltpu.SMEM)
    vmem = pl.BlockSpec(memory_space=pltpu.VMEM)
    return pl.pallas_call(
        kernel,
        out_shape=[jax.ShapeDtypeStruct((half, LANES), jnp.float32)] * 2,
        in_specs=[smem] * 4 + [vmem] * 2,
        out_specs=[vmem] * 2,
        scratch_shapes=[
            pltpu.VMEM(init.shape, jnp.float32),
            pltpu.VMEM((angles * qcount, tiles, LANES), jnp.float32),
        ],
        compiler_params=pltpu.CompilerParams(vmem_limit_bytes=VMEM_LIMIT // 4),
        cost_estimate=pl.CostEstimate(flops=COST, bytes_accessed=COST, transcendentals=0),
        name="other_images",
    )(*listing, dirs, rock, strain, init)


def resolve(unit, total, blocks, parts):
    cols = blocks[0].shape[1]
    vmem = pl.BlockSpec(memory_space=pltpu.VMEM)
    before = () if total is None else (total,)

    def kernel(*refs):
        block_refs, part_refs, out_ref = refs[: len(blocks)], refs[len(blocks) : len(blocks) + len(parts)], refs[-1]
        values = [
            part[pl.ds(start, unit), :] for part in part_refs for start in range(0, part.shape[0], unit)
        ]
        value = jnp.concatenate(values, axis=1)
        block = jnp.concatenate([ref[...] for ref in block_refs], axis=0)
        high = value.astype(jnp.bfloat16)
        low = (value - high.astype(jnp.float32)).astype(jnp.bfloat16)
        sums = jnp.dot(high, block, preferred_element_type=jnp.float32) + jnp.dot(
            low, block, preferred_element_type=jnp.float32
        )
        out_ref[...] = sums if total is None else sums + refs[-2][...]

    return pl.pallas_call(
        kernel,
        out_shape=jax.ShapeDtypeStruct((unit, cols), jnp.float32),
        in_specs=[vmem] * (len(blocks) + len(parts) + len(before)),
        out_specs=vmem,
        compiler_params=pltpu.CompilerParams(vmem_limit_bytes=VMEM_LIMIT),
        cost_estimate=pl.CostEstimate(flops=COST, bytes_accessed=COST, transcendentals=0),
        name="resolve",
    )(*blocks, *parts, *before)


def bit(value, number):
    return (value >> number) & 1


def listing(info, me, raw, halves, angles, units):
    tiles = info.shape[1]
    owner = info // ROWS
    keep = bit(owner, raw) == bit(me, raw)
    position = jnp.zeros_like(owner)
    for number in halves:
        position = 2 * position + (bit(owner, number) == bit(me, number)).astype(jnp.int32)
    target = (position * angles + jnp.arange(angles)[:, None]) * ROWS + info % ROWS
    number = jnp.arange(tiles)
    earlier = keep[:, None, :] & (number[None, None, :] < number[None, :, None])
    rank = jnp.where(keep, jnp.sum(earlier.astype(jnp.int32), axis=2), -1)
    code = number[None, :] + tiles * (target - units)
    lists = tiles * units + jnp.sum(
        jnp.where(rank[:, None, :] == number[None, :, None], code[:, None, :], 0), axis=2
    )
    return jnp.sum(keep.astype(jnp.int32), axis=1), lists


def by_images(strain, dest, det_row, dirs, rock_angles, resolution):
    slabs = lax.axis_size("slab")
    rock_size = lax.axis_size("rock")
    tiles = strain.shape[0]
    pix = resolution.shape[1]
    rocks = rock_angles.shape[0]
    angles, qcount, comps = dirs.shape
    norm = ROWS / (QDIR * DEPTH * TILES_DEV)
    bits = slabs.bit_length() - 1
    unit = angles * ROWS * rocks
    units = slabs // 2 * angles * ROWS
    image_rows = units * rocks
    me = lax.axis_index("slab")
    chunks = pix // LANES

    odd = lax.axis_index("rock") & 1

    def swap(value, number, axis="slab"):
        if axis == "slab" and number[0] != number[1]:
            pairs = [
                (i * rock_size + j, (i ^ (1 << number[j & 1])) * rock_size + j)
                for i in range(slabs)
                for j in range(rock_size)
            ]
            return lax.ppermute(value, ("slab", "rock"), pairs)
        number = number[0] if axis == "slab" else number
        return lax.ppermute(value, axis, [(i, i ^ (1 << number)) for i in range(lax.axis_size(axis))])

    same = [(k, k) for k in range(bits)]
    plans = [(same[0], tuple(same[1:])), ((1, 0), ((0, 1),) + tuple(same[2:]))]
    plan_of = [1] * (chunks - 1) + [0]
    every = list(range(chunks))
    launches = every
    last = []

    def tie(value):
        return lax.optimization_barrier((value, *last))[0]

    def mark(value):
        last[:] = [value]
        return value

    info = dest[:, :, 0] * ROWS + det_row
    info_rows = angles * tiles // LANES
    padded = jnp.pad(info.astype(jnp.float32).reshape(info_rows, LANES), ((0, -info_rows % GROUP), (0, 0)))
    by_comp = strain.transpose(1, 0, 2).reshape(comps * tiles // GROUP, GROUP, pix)
    padded = padded.reshape(-1, GROUP, LANES)
    own = {}
    other = {}

    def piece(source, c):
        block = source[:, :, c * LANES : (c + 1) * LANES]
        if plan_of[c] in plan_of[:c]:
            return block
        return jnp.concatenate([block, padded], axis=0)

    def launch(c):
        own[c] = mark(tie(pieces[c]) if last else pieces[c])
        other[c] = swap(own[c], plans[plan_of[c]][0])

    pieces = {0: piece(by_comp, 0)}
    launch(0)
    source = tie(by_comp)
    pieces.update({c: piece(source, c) for c in every[1:]})
    if chunks > 1:
        launch(1)
    used = sorted(set(plan_of))

    def numbers(k):
        raw, halves = plans[k]
        pick = lambda pair: pair[0] if pair[0] == pair[1] else jnp.where(odd == 1, pair[1], pair[0])
        return pick(raw), [pick(pair) for pair in halves]

    own_list = {k: listing(tie(info), me, *numbers(k), angles, units) for k in used}
    other_list = {}

    def learn(c):
        arrived = mark(tie(other[c]))
        below = arrived[by_comp.shape[0] :].reshape(-1, LANES)[:info_rows]
        below = below.reshape(angles, tiles).astype(jnp.int32)
        other_list[plan_of[c]] = listing(below, me, *numbers(plan_of[c]), angles, units)

    partial = {}
    held = {}
    flying = {}
    half = image_rows // 2

    def begin(*group):
        kinds = sorted({plan_of[c] for c in group})
        found = own_images(
            [kinds.index(plan_of[c]) for c in group],
            [own_list[k] for k in kinds],
            dirs,
            rock_angles,
            [tie(own[group[0]])] + [own[c] for c in group[1:]],
            tiles,
            image_rows + rocks,
        )
        partial.update(zip(group, found))
        mark(found[0])

    def first(c):
        k = plan_of[c]
        if k not in other_list:
            learn(c)
        sent, held[c] = other_images(other_list[k], dirs, rock_angles, tie(other[c]), partial[c], tiles, half, norm)
        mark(sent)
        flying[c] = swap(sent, plans[k][1][0])

    def middle(c):
        arrived = tie(flying[c])
        for number in plans[plan_of[c]][1][1:]:
            rows = held[c].shape[0] // 2
            sent = mark(held[c][:rows] + arrived[:rows])
            flying[c] = swap(sent, number)
            held[c] = held[c][rows:] + arrived[rows:]
            arrived = flying[c]

    lower = list(reversed(range(max(rock_size.bit_length() - 2, 0))))
    image = {}
    beside = {}

    def spread(part):
        found = [part]
        for number in lower:
            found = [x for p in found for x in (p, swap(p, number, "rock"))]
        return found

    def final(c):
        image[c] = mark(held[c] + tie(flying[c]))
        if rock_size > 1:
            beside[c] = swap(image[c], len(lower), "rock")

    def arrive(c):
        if rock_size > 1:
            beside[c] = mark(tie(beside[c]))

    def join(values):
        return jnp.concatenate(values, axis=0) if len(values) > 1 else values[0]

    rock_index = lax.axis_index("rock")
    found = {}
    blocks = {}
    result = []

    def near(*group):
        found[group] = spread(mark(join([image[c] for c in group])))

    def far(*group):
        if rock_size > 1:
            found[group] = found[group] + spread(mark(tie(join([beside[c] for c in group]))))

    def rows(*group):
        source = tie(resolution)
        places = [(rock_index ^ j) * pix + c * LANES for j in range(rock_size) for c in group]
        blocks[group] = [lax.dynamic_slice(source, (at, 0), (LANES, resolution.shape[1])) for at in places]
        mark(blocks[group][-1])

    def multiply(*group):
        parts = found[group]
        total = result[-1] if result else None
        result.append(mark(resolve(unit, total, blocks[group], [tie(parts[0])] + parts[1:])))

    if plan_of == list(SCHEDULED):
        steps = SCHEDULE
    else:
        steps = [("launch", c) for c in every[2:]] + [("begin", *every)] + [(name, c) for name in ("first", "middle", "final") for c in every]
        steps += [("rows", *every), ("near", *every), ("far", *every), ("multiply", *every)]
    doing = dict(begin=begin, first=first, middle=middle, final=final, arrive=arrive, near=near, far=far, rows=rows)
    doing["multiply"] = multiply
    doing["launch"] = launch
    doing["wait"] = lambda c: other.update({c: mark(tie(other[c]))})
    for name, *group in steps:
        doing[name](*group)
    return result[-1].reshape(angles, ROWS, rocks, pix)


def local(strain, dest, det_row, dirs, rock_angles, resolution):
    slabs = lax.axis_size("slab")
    rock_size = lax.axis_size("rock")
    tiles, unused, vox = strain.shape
    pix = resolution.shape[1]
    slots = slabs * (2 * tiles // slabs)
    images_smaller = slabs * ROWS * rock_angles.shape[0] * pix <= slots * dirs.shape[1] * vox
    powers = all(size & (size - 1) == 0 for size in (slabs, rock_size, tiles))
    regular = powers and slabs >= 4 and tiles % LANES == 0 and vox == pix and pix % LANES == 0
    plan = by_images if images_smaller and regular else by_tiles
    return plan(strain, dest, det_row, dirs, rock_angles, resolution)


def solution(mesh):
    placed = (
        P("slab", None, "rock"),
        P(None, "slab", None),
        P(None, "slab"),
        P(),
        P(),
        P(None, "rock"),
    )
    return jax.shard_map(
        local, mesh=mesh, in_specs=placed, out_specs=P(None, "slab", None, "rock"), check_vma=False
    )
```

```python
import math
import jax
import jax.numpy as jnp
from jax import lax
from jax.experimental import pallas as pl
from jax.experimental.pallas import tpu as pltpu
from jax.sharding import PartitionSpec as P

TILES_DEV = 128
DEPTH = 1
QDIR = 4
ROWS = 8
ANGLES = 2
LANES = 128
GROUP = 8
VMEM_LIMIT = 12 * 1024 * 1024
COST = 1024
SCHEDULE = (
    ("begin", 0, 1),
    ("launch", 2),
    ("first", 0),
    ("first", 1),
    ("launch", 3),
    ("begin", 2, 3),
    ("middle", 0),
    ("first", 2),
    ("rows", 0, 1),
    ("rows", 2, 3),
    ("middle", 1),
    ("first", 3),
    ("final", 0),
    ("middle", 2),
    ("arrive", 0),
    ("final", 1),
    ("middle", 3),
    ("final", 2),
    ("arrive", 1),
    ("near", 0, 1),
    ("far", 0, 1),
    ("final", 3),
    ("multiply", 0, 1),
    ("near", 2, 3),
    ("arrive", 2),
    ("far", 2, 3),
    ("multiply", 2, 3),
)
SCHEDULED = (1, 1, 1, 0)
SCALE = math.sqrt(0.5 / math.log(2.0))


def by_tiles(strain, dest, det_row, dirs, rock_angles, resolution):
    slabs = lax.axis_size("slab")
    tiles_here = strain.shape[0]
    vox_here = strain.shape[2]
    pix_here = resolution.shape[1]
    depth = vox_here // pix_here
    capacity = 2 * tiles_here // slabs
    slots = slabs * capacity
    block_size = 64
    rocks = rock_angles.shape[0]
    qcount = dirs.shape[1]
    norm = ROWS / (QDIR * DEPTH * TILES_DEV)
    row_ids = jnp.arange(ROWS, dtype=jnp.float32)
    lower = lax.broadcasted_iota(jnp.int32, (tiles_here, tiles_here), 1) < lax.broadcasted_iota(
        jnp.int32, (tiles_here, tiles_here), 0
    )

    def add_block(total, item):
        proj_block, row_block = item
        inten = jnp.sum(
            jnp.exp(-0.5 * (proj_block[:, :, None, :] - rock_angles[None, None, :, None]) ** 2),
            axis=1,
        )
        summed = inten.reshape(block_size, rocks, pix_here, depth).sum(axis=3)
        onehot = (row_ids[:, None] == row_block[None, :]).astype(jnp.float32)
        added = jnp.dot(
            onehot, summed.reshape(block_size, rocks * pix_here), precision=lax.Precision.HIGHEST
        )
        return (total + added, None)

    images = []
    for angle in range(ANGLES):
        owner = dest[angle, :, 0]
        same = (owner[:, None] == owner[None, :]) & lower
        rank = jnp.sum(same.astype(jnp.int32), axis=1)
        slot = owner * capacity + rank
        row_send = (
            jnp.full((slots,), -1.0, jnp.float32).at[slot].set(det_row[angle].astype(jnp.float32))
        )
        row_send = row_send.reshape(slabs, capacity)
        weights = dirs[angle]
        local_proj = jnp.einsum("qc,tcv->tqv", weights, strain, precision=lax.Precision.HIGHEST)
        outgoing = jnp.zeros((slots, qcount, vox_here), jnp.float32).at[slot].set(local_proj)
        outgoing = outgoing.reshape(slabs, capacity, qcount, vox_here)
        arrived, arrived_rows = (
            lax.all_to_all(outgoing, "slab", split_axis=0, concat_axis=0, tiled=True),
            lax.all_to_all(row_send, "slab", split_axis=0, concat_axis=0, tiled=True),
        )
        proj = arrived.reshape(slots, qcount, vox_here)
        proj_blocks = proj.reshape(slots // block_size, block_size, qcount, vox_here)
        row_blocks = arrived_rows.reshape(slots // block_size, block_size)
        image, unused = lax.scan(
            add_block, jnp.zeros((ROWS, rocks * pix_here), jnp.float32), (proj_blocks, row_blocks)
        )
        images.append(image.reshape(ROWS, rocks, pix_here) * norm)
    stacked = jnp.stack(images, axis=0)
    columns = resolution.astype(jnp.float32)
    return jnp.einsum(
        "agrp,pk->agrk",
        lax.all_gather(stacked, "rock", axis=3, tiled=True),
        columns,
        precision=lax.Precision.HIGHEST,
    )


def prepared_rocks(rock_ref):
    rocks = rock_ref.shape[0]
    row = lax.broadcasted_iota(jnp.int32, (rocks, LANES), 0)
    rock = jnp.zeros((rocks, LANES), jnp.float32)
    for i in range(rocks):
        rock = jnp.where(row == i, rock_ref[i] * SCALE, rock)
    return rock


def add_tiles(count_ref, list_ref, dirs_ref, rock, strain_ref, proj, acc):
    angles, qcount, comps = dirs_ref.shape
    tiles, lanes = proj.shape[1:]
    rocks = rock.shape[0]
    step = 4 * GROUP
    twice = rock + rock
    for k in range(angles * qcount):
        scaled = [dirs_ref[k // qcount, k % qcount, c] * SCALE for c in range(comps)]
        for start in range(0, tiles, step):
            total = None
            for c in range(comps):
                part = strain_ref[pl.ds((c * tiles + start) // GROUP, step // GROUP)] * scaled[c]
                total = part if total is None else total + part
            proj[k, pl.ds(start, step), :] = total.reshape(step, lanes)

    for angle in range(angles):

        @pl.loop(0, (count_ref[angle] + GROUP - 1) // GROUP)
        def _(block):
            sums = []
            targets = []
            for j in range(GROUP):
                code = list_ref[angle, block * GROUP + j]
                tile = code & (tiles - 1)
                target = (code >> (tiles - 1).bit_length()) * rocks
                targets.append(pl.multiple_of(target, rocks))
                total = None
                for q in range(qcount):
                    p = jnp.broadcast_to(proj[angle * qcount + q, pl.ds(tile, 1), :], (rocks, lanes))
                    e = jnp.exp2(p * (twice - p))
                    total = e if total is None else total + e
                sums.append(total)
            for target, total in zip(targets, sums):
                acc[pl.ds(target, rocks), :] += total


def own_images(plan_of, listings, dirs, rock, strains, tiles, rows):
    used = len(listings)
    count = len(strains)
    angles, qcount, comps = dirs.shape

    def kernel(*refs):
        list_refs = refs[: 2 * used]
        dirs_ref, rock_ref = refs[2 * used : 2 * used + 2]
        strain_refs = refs[2 * used + 2 : 2 * used + 2 + count]
        outs, proj = refs[-1 - count : -1], refs[-1]
        rock = prepared_rocks(rock_ref)
        for c in range(count):
            k = plan_of[c]
            outs[c][...] = jnp.zeros_like(outs[c])
            add_tiles(list_refs[2 * k], list_refs[2 * k + 1], dirs_ref, rock, strain_refs[c], proj, outs[c])

    smem = pl.BlockSpec(memory_space=pltpu.SMEM)
    vmem = pl.BlockSpec(memory_space=pltpu.VMEM)
    return pl.pallas_call(
        kernel,
        out_shape=[jax.ShapeDtypeStruct((rows, LANES), jnp.float32)] * count,
        in_specs=[smem] * (2 * used + 2) + [vmem] * count,
        out_specs=[vmem] * count,
        scratch_shapes=[pltpu.VMEM((angles * qcount, tiles, LANES), jnp.float32)],
        compiler_params=pltpu.CompilerParams(vmem_limit_bytes=VMEM_LIMIT // 2),
        cost_estimate=pl.CostEstimate(flops=COST, bytes_accessed=COST, transcendentals=0),
        name="own_images",
    )(*[x for listing in listings for x in listing], dirs, rock, *strains)


def other_images(listing, dirs, rock, strain, init, tiles, half, norm):
    angles, qcount, comps = dirs.shape
    rocks = rock.shape[0]

    def kernel(count_ref, list_ref, dirs_ref, rock_ref, strain_ref, init_ref, sent_ref, kept_ref, acc, proj):
        rock = prepared_rocks(rock_ref)
        acc[...] = init_ref[...]
        add_tiles(count_ref, list_ref, dirs_ref, rock, strain_ref, proj, acc)
        factor = jnp.exp2(-(rock * rock)) * norm
        for start, out in ((0, sent_ref), (half, kept_ref)):
            for row in range(0, half, rocks):
                out[pl.ds(row, rocks), :] = acc[pl.ds(start + row, rocks), :] * factor

    smem = pl.BlockSpec(memory_space=pltpu.SMEM)
    vmem = pl.BlockSpec(memory_space=pltpu.VMEM)
    return pl.pallas_call(
        kernel,
        out_shape=[jax.ShapeDtypeStruct((half, LANES), jnp.float32)] * 2,
        in_specs=[smem] * 4 + [vmem] * 2,
        out_specs=[vmem] * 2,
        scratch_shapes=[
            pltpu.VMEM(init.shape, jnp.float32),
            pltpu.VMEM((angles * qcount, tiles, LANES), jnp.float32),
        ],
        compiler_params=pltpu.CompilerParams(vmem_limit_bytes=VMEM_LIMIT // 4),
        cost_estimate=pl.CostEstimate(flops=COST, bytes_accessed=COST, transcendentals=0),
        name="other_images",
    )(*listing, dirs, rock, strain, init)


def resolve(unit, total, blocks, parts):
    cols = blocks[0].shape[1]
    vmem = pl.BlockSpec(memory_space=pltpu.VMEM)
    before = () if total is None else (total,)

    def kernel(*refs):
        block_refs, part_refs, out_ref = refs[: len(blocks)], refs[len(blocks) : len(blocks) + len(parts)], refs[-1]
        values = [
            part[pl.ds(start, unit), :] for part in part_refs for start in range(0, part.shape[0], unit)
        ]
        value = jnp.concatenate(values, axis=1)
        block = jnp.concatenate([ref[...] for ref in block_refs], axis=0)
        high = value.astype(jnp.bfloat16)
        low = (value - high.astype(jnp.float32)).astype(jnp.bfloat16)
        sums = jnp.dot(high, block, preferred_element_type=jnp.float32) + jnp.dot(
            low, block, preferred_element_type=jnp.float32
        )
        out_ref[...] = sums if total is None else sums + refs[-2][...]

    return pl.pallas_call(
        kernel,
        out_shape=jax.ShapeDtypeStruct((unit, cols), jnp.float32),
        in_specs=[vmem] * (len(blocks) + len(parts) + len(before)),
        out_specs=vmem,
        compiler_params=pltpu.CompilerParams(vmem_limit_bytes=VMEM_LIMIT),
        cost_estimate=pl.CostEstimate(flops=COST, bytes_accessed=COST, transcendentals=0),
        name="resolve",
    )(*blocks, *parts, *before)


def bit(value, number):
    return (value >> number) & 1


def listing(info, me, raw, halves, angles, units):
    tiles = info.shape[1]
    owner = info // ROWS
    keep = bit(owner, raw) == bit(me, raw)
    position = jnp.zeros_like(owner)
    for number in halves:
        position = 2 * position + (bit(owner, number) == bit(me, number)).astype(jnp.int32)
    target = (position * angles + jnp.arange(angles)[:, None]) * ROWS + info % ROWS
    number = jnp.arange(tiles)
    earlier = keep[:, None, :] & (number[None, None, :] < number[None, :, None])
    rank = jnp.where(keep, jnp.sum(earlier.astype(jnp.int32), axis=2), -1)
    code = number[None, :] + tiles * (target - units)
    lists = tiles * units + jnp.sum(
        jnp.where(rank[:, None, :] == number[None, :, None], code[:, None, :], 0), axis=2
    )
    return jnp.sum(keep.astype(jnp.int32), axis=1), lists


def by_images(strain, dest, det_row, dirs, rock_angles, resolution):
    slabs = lax.axis_size("slab")
    rock_size = lax.axis_size("rock")
    tiles = strain.shape[0]
    pix = resolution.shape[1]
    rocks = rock_angles.shape[0]
    angles, qcount, comps = dirs.shape
    norm = ROWS / (QDIR * DEPTH * TILES_DEV)
    bits = slabs.bit_length() - 1
    unit = angles * ROWS * rocks
    units = slabs // 2 * angles * ROWS
    image_rows = units * rocks
    me = lax.axis_index("slab")
    chunks = pix // LANES

    odd = lax.axis_index("rock") & 1

    def swap(value, number, axis="slab"):
        if axis == "slab" and number[0] != number[1]:
            pairs = [
                (i * rock_size + j, (i ^ (1 << number[j & 1])) * rock_size + j)
                for i in range(slabs)
                for j in range(rock_size)
            ]
            return lax.ppermute(value, ("slab", "rock"), pairs)
        number = number[0] if axis == "slab" else number
        return lax.ppermute(value, axis, [(i, i ^ (1 << number)) for i in range(lax.axis_size(axis))])

    same = [(k, k) for k in range(bits)]
    plans = [(same[0], tuple(same[1:])), ((1, 0), ((0, 1),) + tuple(same[2:]))]
    plan_of = [1] * (chunks - 1) + [0]
    every = list(range(chunks))
    launches = every
    last = []

    def tie(value):
        return lax.optimization_barrier((value, *last))[0]

    def mark(value):
        last[:] = [value]
        return value

    info = dest[:, :, 0] * ROWS + det_row
    info_rows = angles * tiles // LANES
    padded = jnp.pad(info.astype(jnp.float32).reshape(info_rows, LANES), ((0, -info_rows % GROUP), (0, 0)))
    by_comp = strain.transpose(1, 0, 2).reshape(comps * tiles // GROUP, GROUP, pix)
    padded = padded.reshape(-1, GROUP, LANES)
    own = {}
    other = {}

    def piece(source, c):
        block = source[:, :, c * LANES : (c + 1) * LANES]
        if plan_of[c] in plan_of[:c]:
            return block
        return jnp.concatenate([block, padded], axis=0)

    def launch(c):
        own[c] = mark(tie(pieces[c]) if last else pieces[c])
        other[c] = swap(own[c], plans[plan_of[c]][0])

    pieces = {0: piece(by_comp, 0)}
    launch(0)
    source = tie(by_comp)
    pieces.update({c: piece(source, c) for c in every[1:]})
    if chunks > 1:
        launch(1)
    used = sorted(set(plan_of))

    def numbers(k):
        raw, halves = plans[k]
        pick = lambda pair: pair[0] if pair[0] == pair[1] else jnp.where(odd == 1, pair[1], pair[0])
        return pick(raw), [pick(pair) for pair in halves]

    own_list = {k: listing(tie(info), me, *numbers(k), angles, units) for k in used}
    other_list = {}

    def learn(c):
        arrived = mark(tie(other[c]))
        below = arrived[by_comp.shape[0] :].reshape(-1, LANES)[:info_rows]
        below = below.reshape(angles, tiles).astype(jnp.int32)
        other_list[plan_of[c]] = listing(below, me, *numbers(plan_of[c]), angles, units)

    partial = {}
    held = {}
    flying = {}
    half = image_rows // 2

    def begin(*group):
        kinds = sorted({plan_of[c] for c in group})
        found = own_images(
            [kinds.index(plan_of[c]) for c in group],
            [own_list[k] for k in kinds],
            dirs,
            rock_angles,
            [tie(own[group[0]])] + [own[c] for c in group[1:]],
            tiles,
            image_rows + rocks,
        )
        partial.update(zip(group, found))
        mark(found[0])

    def first(c):
        k = plan_of[c]
        if k not in other_list:
            learn(c)
        sent, held[c] = other_images(other_list[k], dirs, rock_angles, tie(other[c]), partial[c], tiles, half, norm)
        mark(sent)
        flying[c] = swap(sent, plans[k][1][0])

    def middle(c):
        arrived = tie(flying[c])
        for number in plans[plan_of[c]][1][1:]:
            rows = held[c].shape[0] // 2
            sent = mark(held[c][:rows] + arrived[:rows])
            flying[c] = swap(sent, number)
            held[c] = held[c][rows:] + arrived[rows:]
            arrived = flying[c]

    lower = list(reversed(range(max(rock_size.bit_length() - 2, 0))))
    image = {}
    beside = {}

    def spread(part):
        found = [part]
        for number in lower:
            found = [x for p in found for x in (p, swap(p, number, "rock"))]
        return found

    def final(c):
        image[c] = mark(held[c] + tie(flying[c]))
        if rock_size > 1:
            beside[c] = swap(image[c], len(lower), "rock")

    def arrive(c):
        if rock_size > 1:
            beside[c] = mark(tie(beside[c]))

    def join(values):
        return jnp.concatenate(values, axis=0) if len(values) > 1 else values[0]

    rock_index = lax.axis_index("rock")
    found = {}
    blocks = {}
    result = []

    def near(*group):
        found[group] = spread(mark(join([image[c] for c in group])))

    def far(*group):
        if rock_size > 1:
            found[group] = found[group] + spread(mark(tie(join([beside[c] for c in group]))))

    def rows(*group):
        source = tie(resolution)
        places = [(rock_index ^ j) * pix + c * LANES for j in range(rock_size) for c in group]
        blocks[group] = [lax.dynamic_slice(source, (at, 0), (LANES, resolution.shape[1])) for at in places]
        mark(blocks[group][-1])

    def multiply(*group):
        parts = found[group]
        total = result[-1] if result else None
        result.append(mark(resolve(unit, total, blocks[group], [tie(parts[0])] + parts[1:])))

    if plan_of == list(SCHEDULED):
        steps = SCHEDULE
    else:
        steps = [("launch", c) for c in every[2:]] + [("begin", *every)] + [(name, c) for name in ("first", "middle", "final") for c in every]
        steps += [("rows", *every), ("near", *every), ("far", *every), ("multiply", *every)]
    doing = dict(begin=begin, first=first, middle=middle, final=final, arrive=arrive, near=near, far=far, rows=rows)
    doing["multiply"] = multiply
    doing["launch"] = launch
    doing["wait"] = lambda c: other.update({c: mark(tie(other[c]))})
    for name, *group in steps:
        doing[name](*group)
    return result[-1].reshape(angles, ROWS, rocks, pix)


def local(strain, dest, det_row, dirs, rock_angles, resolution):
    slabs = lax.axis_size("slab")
    rock_size = lax.axis_size("rock")
    tiles, unused, vox = strain.shape
    pix = resolution.shape[1]
    slots = slabs * (2 * tiles // slabs)
    images_smaller = slabs * ROWS * rock_angles.shape[0] * pix <= slots * dirs.shape[1] * vox
    powers = all(size & (size - 1) == 0 for size in (slabs, rock_size, tiles))
    regular = powers and slabs >= 4 and tiles % LANES == 0 and vox == pix and pix % LANES == 0
    plan = by_images if images_smaller and regular else by_tiles
    return plan(strain, dest, det_row, dirs, rock_angles, resolution)


def solution(mesh):
    placed = (
        P("slab", None, "rock"),
        P(None, "slab", None),
        P(None, "slab"),
        P(),
        P(),
        P(None, "rock"),
    )
    return jax.shard_map(
        local, mesh=mesh, in_specs=placed, out_specs=P(None, "slab", None, "rock"), check_vma=False
    )
```
